32 devices in a mesh: row: 4 (over y, x), col: 8 (over z, core).
Axes of the slice: x: 2, y: 2, z: 4, core: 2. Of those that a mesh axis runs over, the one named last changes fastest.
Arguments:
- panel: bfloat16 [15, 8, 512, 512], P(None, 'row', 'col'), may hold values from -0.109375 to 0.109375
- diag_inverse: float32 [6, 8, 512, 512], P(None, 'row', 'col'), as said below
- parents: int32 [5, 8], replicated, may hold values from 0 to 7, as said below
- supernode_sizes: int32 [6, 8], replicated, may hold values from 128 to 512
Outputs:
- cross: float32 [15, 8, 512, 512], P(None, 'row', 'col')
- marginal: float32 [6, 8, 512, 512], P(None, 'row', 'col')
The draws below stay inside these ranges and needn't reach their ends.
Inputs may be any that keep to these rules, and one draw needn't show every extreme that they name: `parents`: the parent of a supernode g of level d + 1 is a supernode of level d whose index divided by 2 equals g divided by 2, or that minus 1 modulo 8 / 2. `diag_inverse`: every block is symmetric and positive definite.
All inputs are finite; a program needn't handle non-finite values.
Results may differ from the reference program's by a relative error of at most 0.0023.
Values may be sent and summed in bfloat16 or wider, within the bound.
No kernel may reach another device: no remote copies, remote signals or barrier semaphores. Data moves between devices by JAX's collectives and lax.ppermute only.
A program may use at most 128 MiB of HBM per device.

```python
import jax
import jax.numpy as jnp
from jax import lax

W = 512
LEVELS = 6
NPR = 2
NODES = 8
PAIRS = 15


def draw_diag_inverse(key, part):
    first = jax.random.fold_in(jax.random.fold_in(key, 11), 0)
    basis = jax.random.normal(first, (LEVELS, NODES, W, W), jnp.float32)
    gram = jnp.einsum('abij,abkj->abik', basis, basis, precision=lax.Precision.HIGHEST) / (2.0 * W)
    gram = 0.5 * (gram + jnp.swapaxes(gram, 2, 3)) + 0.5 * jnp.eye(W, dtype=jnp.float32)[None, None]
    return gram


def draw_parents(key, part):
    first, second, third = jax.random.split(jax.random.fold_in(key, 23), 3)
    indices = jnp.arange(NODES, dtype=jnp.int32)
    row_count = NODES // NPR
    own_rows = indices // NPR
    side = jax.random.randint(first, (LEVELS - 1, NODES), 0, 2, jnp.int32)
    within = jnp.minimum(jax.random.randint(second, (LEVELS - 1, NODES), 0, NPR, jnp.int32), jax.random.randint(third, (LEVELS - 1, NODES), 0, NPR, jnp.int32))
    source_rows = (own_rows[None, :] - side + row_count) % row_count
    return (source_rows * NPR + within).astype(jnp.int32)


def plant(entries, stream_key, low, top_value):
    longest = entries.shape.index(max(entries.shape))
    spots = []
    for shift in (0, 1):
        where = [jax.random.randint(jax.random.fold_in(stream_key, axis), (), 0, length) for axis, length in enumerate(entries.shape)]
        where[longest] = (where[longest] + shift) % entries.shape[longest]
        spots.append(tuple(where))
    return entries.at[spots[0]].set(low).at[spots[1]].set(top_value)


def levels(stream_key, extent, cuts, least, largest):
    def one(position, shards_of):
        steps = jax.random.uniform(jax.random.fold_in(jax.random.fold_in(stream_key, 6), position), (shards_of,), jnp.float32, least / len(cuts), largest / len(cuts))
        return jnp.repeat(jnp.exp(steps), extent[position] // shards_of).reshape((-1,) + (1,) * (len(extent) - position - 1))

    loudness = one(*cuts[0])
    for cut in cuts[1:]:
        loudness = loudness * one(*cut)
    return loudness


def scatter_about(stream_key, dims, width, most, shards=(), kind=jnp.bfloat16):
    drawn = jax.random.normal(stream_key, dims, jnp.float32) * width
    if len(shards) > 0:
        drawn = levels(stream_key, dims, shards, -0.22, 0.18) * drawn
    return jnp.clip(drawn, min=-most, max=most).astype(kind)


def setup_inputs(seed: int = 0) -> dict:
    seeds = jax.random.split(jax.random.key(seed), 5)
    panel = scatter_about(seeds[0], (PAIRS, NODES, W, W), (W * LEVELS) ** -0.5, 0.109375, ((1, 4), (2, 8)))
    diag_inverse = draw_diag_inverse(jax.random.fold_in(seeds[4], 71), 0)
    parents = draw_parents(jax.random.fold_in(seeds[4], 71), 0)
    supernode_sizes = plant(jax.random.randint(seeds[3], (LEVELS, NODES), W // 4, W + 1), jax.random.fold_in(seeds[3], 1), W // 4, W).astype(jnp.int32)
    return dict(panel=panel, diag_inverse=diag_inverse, parents=parents, supernode_sizes=supernode_sizes)


def reference(panel, diag_inverse, parents, supernode_sizes):
    columns = jnp.arange(W, dtype=jnp.int32)
    identity = jnp.eye(W, dtype=jnp.float32)
    ancestry_ids = jnp.zeros((0, NODES), jnp.int32)
    crosses = []
    diagonals = []
    chain = None
    for level in range(LEVELS):
        live_cols = (columns[None, :] < supernode_sizes[level][:, None]).astype(jnp.float32)
        diag_base = diag_inverse[level] * live_cols[:, :, None] * live_cols[:, None, :] + identity[None] * (1.0 - live_cols)[:, None, :]
        if level == 0:
            diagonal = diag_base
        else:
            parent_ids = parents[level - 1].astype(jnp.int32)
            ancestry_ids = jnp.concatenate([ancestry_ids[:, parent_ids], parent_ids[None, :]], axis=0)
            upper_sizes = supernode_sizes[jnp.arange(level, dtype=jnp.int32)[:, None], ancestry_ids]
            live_upper = (columns[None, None, :] < upper_sizes[:, :, None]).astype(jnp.float32)
            start = level * (level - 1) // 2
            block = panel[start:start + level].astype(jnp.float32) * live_upper[:, :, :, None] * live_cols[None, :, None, :]
            lower = jnp.transpose(block, (1, 0, 2, 3))
            ancestry = chain[parent_ids]
            cross = -jnp.einsum("nlmik,nmkj->nlij", ancestry, lower, precision=lax.Precision.HIGHEST)
            diagonal = diag_base - jnp.einsum("nlki,nlkj->nij", lower, cross, precision=lax.Precision.HIGHEST)
            crosses.append(jnp.transpose(cross, (1, 0, 2, 3)))
        diagonals.append(diagonal)
        if level < LEVELS - 1:
            if level == 0:
                chain = diagonal[:, None, None]
            else:
                upper = jnp.concatenate([ancestry, cross[:, :, None]], axis=2)
                bottom = jnp.concatenate([jnp.swapaxes(cross, 2, 3)[:, None], diagonal[:, None, None]], axis=2)
                chain = jnp.concatenate([upper, bottom], axis=1)
    return jnp.concatenate(crosses, axis=0), jnp.stack(diagonals)
```

```python
import functools

import jax
import jax.numpy as jnp
from jax import lax
from jax.experimental import pallas as pl
from jax.experimental.pallas import tpu as pltpu
from jax.sharding import PartitionSpec as P

F32 = jnp.float32
BF16 = jnp.bfloat16
F16 = jnp.float16
TOP = 2.0**14
TAIL = 8
VMEM = pl.BlockSpec(memory_space=pltpu.VMEM)
SMEM = pl.BlockSpec(memory_space=pltpu.SMEM)
ANY = pl.BlockSpec(memory_space=pl.ANY)


def factors(peak):
    rows = lax.broadcasted_iota(jnp.int32, (TAIL, peak.shape[1]), 0)
    rest = jnp.maximum(peak, 2.0**-100)
    table = jnp.ones((TAIL, peak.shape[1]), F32)
    whole = jnp.ones_like(rest)
    for i in range(TAIL):
        one = jnp.clip(rest, 2.0**-14, TOP).astype(BF16).astype(F32)
        rest = rest / one
        table = jnp.where(rows == i, jnp.broadcast_to(one, table.shape), table)
        whole = whole * one
    return table, whole


def product(table):
    whole = table[0:1]
    for i in range(1, TAIL):
        whole = whole * table[i : i + 1]
    return whole * (1.0 / TOP)


def peak_of(x):
    down = jnp.max(jnp.abs(x), axis=0, keepdims=True)
    return jnp.broadcast_to(jnp.max(down, axis=1, keepdims=True), down.shape)


def chain_of(parents, level, node):
    found = [None] * level
    for up in range(level - 1, -1, -1):
        node = parents[up, node]
        found[up] = node
    return found


def live_lanes(shape, size):
    return lax.broadcasted_iota(jnp.int32, shape, len(shape) - 1) < size


def base_kernel(npr, rows, width, place, sizes, diag, marginal, message):
    row, col = place[0], place[1]
    for n in range(npr):
        value = diag_base(diag[n], sizes[0, row * npr + n], col * rows, rows, width)
        marginal[n] = value
        table, whole = factors(peak_of(value))
        message[n, :rows] = value * (TOP / whole)
        message[n, rows:] = table


def diag_base(block, size, first, rows, width):
    lines = lax.broadcasted_iota(jnp.int32, (rows, width), 0) + first
    lanes = lax.broadcasted_iota(jnp.int32, (rows, width), 1)
    kept = jnp.where((lines < size) & (lanes < size), block, 0.0)
    return kept + jnp.where((lines == lanes) & (lines >= size), 1.0, 0.0)


def cross_kernel(level, last, spans, n_row, npr, rows, width, *refs):
    place, parents, sizes, panel = refs[:4]
    at = 4
    sources = []
    for up in range(level):
        parts = []
        for _ in range(1 if up == 0 else 2):
            parts.append(refs[at : at + spans[up]])
            at += spans[up]
        sources.append(parts)
    n_out = 2 if last else 3
    outs = refs[at : at + n_out]
    scratch = refs[at + n_out :]
    cross, turn = outs[0], outs[1]
    passed = None if last else outs[2]
    lower, split, panel_sem, block_sem = scratch[:4]
    holders = scratch[4:]
    row = place[0]
    n_col = panel.shape[0]
    high = level * rows

    chains = [chain_of(parents, level, row * npr + n) for n in range(npr)]

    def panel_copy(n, m):
        return pltpu.make_async_copy(panel.at[:, m, n], lower.at[n, m], panel_sem.at[n, m])

    def holder(up, part):
        return holders[0] if up == 0 else holders[1 + 2 * (up - 1) + part]

    for n in range(npr):
        for up in range(level):
            node = chains[n][up]
            back = lax.rem(row - lax.div(node, npr) + n_row, n_row)
            slot = lax.rem(node, npr)
            for part, choices in enumerate(sources[up]):
                for i, source in enumerate(choices):

                    @pl.when(back == i)
                    def _():
                        pltpu.make_async_copy(
                            source.at[slot], holder(up, part).at[n], block_sem.at[n, up, part]
                        ).start()
        for m in range(level):
            panel_copy(n, m).start()

    for n in range(npr):
        for up in range(level):
            size = sizes[up, chains[n][up]]
            for part, choices in enumerate(sources[up]):
                held = holder(up, part)
                pltpu.make_async_copy(choices[0].at[0], held.at[n], block_sem.at[n, up, part]).wait()
                count = (held.shape[1] - TAIL) // rows
                whole = product(held[n, count * rows :])
                for b in range(count):
                    value = held[n, b * rows : (b + 1) * rows] * whole
                    if up > 0 and part == 0:
                        l, m = b, up
                        value = jnp.where(live_lanes(value.shape, size), value, 0.0)
                    else:
                        l, m = up, b
                        value = jnp.where(
                            live_lanes(value.shape, sizes[m, chains[n][m]]), value, 0.0
                        )
                    top = value.astype(BF16)
                    split[n, m, l * rows : (l + 1) * rows] = top
                    split[n, m, high + l * rows : high + (l + 1) * rows] = (
                        value - top.astype(F32)
                    ).astype(BF16)

    results = []
    for n in range(npr):
        total = None
        for m in range(level):
            panel_copy(n, m).wait()
            block = lower[n, m].reshape(width, width)
            term = jnp.dot(split[n, m], block, preferred_element_type=F32)
            total = term if total is None else total + term
        value = -(total[:high] + total[high:])
        value = jnp.where(live_lanes(value.shape, sizes[level, row * npr + n]), value, 0.0)
        for l in range(level):
            cross[l, n] = value[l * rows : (l + 1) * rows]
        table, whole = factors(peak_of(value))
        value = value * (TOP / whole)
        if not last:
            passed[n, :high] = value
            passed[n, high:] = table
        results.append((value, table))
    for c in range(n_col):
        piece = slice(c * rows, (c + 1) * rows)
        turn[c, :high] = jnp.concatenate([v[:, piece] for v, _ in results], axis=1)
        turn[c, high:] = jnp.concatenate([t[:, piece] for _, t in results], axis=1)


def marginal_kernel(level, last, n_row, npr, rows, width, *refs):
    place, sizes, panel, turned, diag = refs[:5]
    n_out = 1 if last else 2
    outs = refs[5 : 5 + n_out]
    lower, panel_sem = refs[5 + n_out :]
    marginal = outs[0]
    message = None if last else outs[1]
    row, col = place[0], place[1]
    n_col = panel.shape[0]
    high = level * rows

    def panel_copy(n, m):
        return pltpu.make_async_copy(panel.at[:, m, n], lower.at[n, m], panel_sem.at[n, m])

    for m in range(level):
        for n in range(npr):
            panel_copy(n, m).start()

    scales = jnp.concatenate(
        [jnp.broadcast_to(product(turned[c, high:]), (rows, npr * rows)) for c in range(n_col)], axis=0
    )
    totals = [None] * npr
    sides = [[] for _ in range(npr)]
    for l in range(level):
        upright = turned[:, l * rows : (l + 1) * rows].reshape(width, npr * rows) * scales
        flat = upright.T
        top = flat.astype(BF16)
        low = (flat - top.astype(F32)).astype(BF16)
        for n in range(npr):
            mine = slice(n * rows, (n + 1) * rows)
            panel_copy(n, l).wait()
            block = lower[n, l].reshape(width, width)
            pair = jnp.concatenate([top[mine], low[mine]], axis=0)
            term = jnp.dot(pair, block, preferred_element_type=F32)
            term = term[:rows] + term[rows:]
            totals[n] = term if totals[n] is None else totals[n] + term
            sides[n].append(flat[mine])
    for n in range(npr):
        size = sizes[level, row * npr + n]
        value = diag_base(diag[n], size, col * rows, rows, width)
        value = value - jnp.where(live_lanes(value.shape, size), totals[n], 0.0)
        marginal[n] = value
        if not last:
            peak = peak_of(value)
            for side in sides[n]:
                peak = jnp.maximum(peak, peak_of(side))
            table, whole = factors(peak)
            scale = TOP / whole
            for l in range(level):
                message[n, l * rows : (l + 1) * rows] = sides[n][l] * scale
            message[n, high : high + rows] = value * scale
            message[n, high + rows :] = table


def params(limit=60 * 2**20):
    return pltpu.CompilerParams(vmem_limit_bytes=limit)


def shards(panel, diag_inverse, parents, supernode_sizes):
    levels, npr, rows, width = diag_inverse.shape
    n_row = lax.axis_size("row")
    n_col = lax.axis_size("col")
    place = jnp.stack([lax.axis_index("row"), lax.axis_index("col")]).astype(jnp.int32)

    def shape(*dims, dtype=F32):
        return jax.ShapeDtypeStruct(dims, dtype)

    def reach(level):
        return min(levels - 1 - level, n_row - 1)

    def spread(message, level):
        found = [message]
        half = message.astype(F16)
        for back in range(1, reach(level) + 1):
            route = [(i, (i + back) % n_row) for i in range(n_row)]
            found.append(lax.ppermute(half, "row", route).astype(F32))
        return found

    whole_panel = []
    for level in range(1, levels):
        start = level * (level - 1) // 2
        whole_panel.append(lax.all_gather(panel[start : start + level], "col", axis=0))

    base, message = pl.pallas_call(
        functools.partial(base_kernel, npr, rows, width),
        out_shape=(shape(npr, rows, width), shape(npr, rows + TAIL, width)),
        in_specs=[SMEM, SMEM, VMEM],
        out_specs=(VMEM, VMEM),
        compiler_params=params(),
        name="base",
    )(place, supernode_sizes, diag_inverse[0])
    crosses = []
    diagonals = [base]
    table = [[spread(message, 0)]]
    for level in range(1, levels):
        last = level == levels - 1
        high = level * rows
        whole = whole_panel[level - 1]
        spans = [min(level - up, n_row - 1) + 1 for up in range(level)]
        sources = [a for up in range(level) for part in table[up] for a in part[: spans[up]]]
        out_shape = [shape(level, npr, rows, width), shape(n_col, high + TAIL, npr * rows)]
        if not last:
            out_shape.append(shape(npr, high + TAIL, width))
        scratch = [
            pltpu.VMEM((npr, level, n_col, rows, width), BF16),
            pltpu.VMEM((npr, level, 2 * high, width), BF16),
            pltpu.SemaphoreType.DMA((npr, level)),
            pltpu.SemaphoreType.DMA((npr, level, 2)),
            pltpu.VMEM((npr, rows + TAIL, width), F32),
        ]
        for up in range(1, level):
            scratch.append(pltpu.VMEM((npr, up * rows + TAIL, width), F32))
            scratch.append(pltpu.VMEM((npr, (up + 1) * rows + TAIL, width), F32))
        made = pl.pallas_call(
            functools.partial(cross_kernel, level, last, spans, n_row, npr, rows, width),
            out_shape=tuple(out_shape),
            in_specs=[SMEM, SMEM, SMEM] + [ANY] * (1 + len(sources)),
            out_specs=(VMEM,) * len(out_shape),
            scratch_shapes=scratch,
            compiler_params=params(),
            name=f"cross{level}",
        )(place, parents, supernode_sizes, whole, *sources)
        crosses.append(made[0])
        ahead = None if last else spread(made[2], level)
        turned = lax.all_to_all(made[1].astype(F16), "col", 0, 0, tiled=True).astype(F32)
        out_shape = [shape(npr, rows, width)]
        if not last:
            out_shape.append(shape(npr, high + rows + TAIL, width))
        done = pl.pallas_call(
            functools.partial(marginal_kernel, level, last, n_row, npr, rows, width),
            out_shape=tuple(out_shape),
            in_specs=[SMEM, SMEM, ANY, VMEM, VMEM],
            out_specs=(VMEM,) * len(out_shape),
            scratch_shapes=[
                pltpu.VMEM((npr, level, n_col, rows, width), BF16),
                pltpu.SemaphoreType.DMA((npr, level)),
            ],
            compiler_params=params(),
            name=f"marginal{level}",
        )(place, supernode_sizes, whole, turned, diag_inverse[level])
        diagonals.append(done[0])
        if not last:
            table.append([ahead, spread(done[1], level)])
    return (jnp.concatenate(crosses, axis=0), jnp.stack(diagonals))


def solution(mesh):
    in_specs = (P(None, "row", "col", None), P(None, "row", "col", None), P(), P())
    out_specs = (P(None, "row", "col", None), P(None, "row", "col", None))
    return jax.shard_map(shards, mesh=mesh, in_specs=in_specs, out_specs=out_specs, check_vma=False)
```

```python
import functools

import jax
import jax.numpy as jnp
from jax import lax
from jax.experimental import pallas as pl
from jax.experimental.pallas import tpu as pltpu
from jax.sharding import PartitionSpec as P

F32 = jnp.float32
BF16 = jnp.bfloat16
F16 = jnp.float16
TOP = 2.0**14
TAIL = 8
VMEM = pl.BlockSpec(memory_space=pltpu.VMEM)
SMEM = pl.BlockSpec(memory_space=pltpu.SMEM)
ANY = pl.BlockSpec(memory_space=pl.ANY)


def factors(peak):
    rows = lax.broadcasted_iota(jnp.int32, (TAIL, peak.shape[1]), 0)
    rest = jnp.maximum(peak, 2.0**-100)
    table = jnp.ones((TAIL, peak.shape[1]), F32)
    whole = jnp.ones_like(rest)
    for i in range(TAIL):
        one = jnp.clip(rest, 2.0**-14, TOP).astype(BF16).astype(F32)
        rest = rest / one
        table = jnp.where(rows == i, jnp.broadcast_to(one, table.shape), table)
        whole = whole * one
    return table, whole


def product(table):
    whole = table[0:1]
    for i in range(1, TAIL):
        whole = whole * table[i : i + 1]
    return whole * (1.0 / TOP)


def peak_of(x):
    down = jnp.max(jnp.abs(x), axis=0, keepdims=True)
    return jnp.broadcast_to(jnp.max(down, axis=1, keepdims=True), down.shape)


def chain_of(parents, level, node):
    found = [None] * level
    for up in range(level - 1, -1, -1):
        node = parents[up, node]
        found[up] = node
    return found


def live_lanes(shape, size):
    return lax.broadcasted_iota(jnp.int32, shape, len(shape) - 1) < size


def base_kernel(npr, rows, width, place, sizes, diag, marginal, message):
    row, col = place[0], place[1]
    for n in range(npr):
        value = diag_base(diag[n], sizes[0, row * npr + n], col * rows, rows, width)
        marginal[n] = value
        table, whole = factors(peak_of(value))
        message[n, :rows] = value * (TOP / whole)
        message[n, rows:] = table


def diag_base(block, size, first, rows, width):
    lines = lax.broadcasted_iota(jnp.int32, (rows, width), 0) + first
    lanes = lax.broadcasted_iota(jnp.int32, (rows, width), 1)
    kept = jnp.where((lines < size) & (lanes < size), block, 0.0)
    return kept + jnp.where((lines == lanes) & (lines >= size), 1.0, 0.0)


def cross_kernel(level, last, spans, n_row, npr, rows, width, *refs):
    place, parents, sizes, panel = refs[:4]
    at = 4
    sources = []
    for up in range(level):
        parts = []
        for _ in range(1 if up == 0 else 2):
            parts.append(refs[at : at + spans[up]])
            at += spans[up]
        sources.append(parts)
    n_out = 2 if last else 3
    outs = refs[at : at + n_out]
    scratch = refs[at + n_out :]
    cross, turn = outs[0], outs[1]
    passed = None if last else outs[2]
    lower, split, panel_sem, block_sem = scratch[:4]
    holders = scratch[4:]
    row = place[0]
    n_col = panel.shape[0]
    high = level * rows

    chains = [chain_of(parents, level, row * npr + n) for n in range(npr)]

    def panel_copy(n, m):
        return pltpu.make_async_copy(panel.at[:, m, n], lower.at[n, m], panel_sem.at[n, m])

    def holder(up, part):
        return holders[0] if up == 0 else holders[1 + 2 * (up - 1) + part]

    for n in range(npr):
        for up in range(level):
            node = chains[n][up]
            back = lax.rem(row - lax.div(node, npr) + n_row, n_row)
            slot = lax.rem(node, npr)
            for part, choices in enumerate(sources[up]):
                for i, source in enumerate(choices):

                    @pl.when(back == i)
                    def _():
                        pltpu.make_async_copy(
                            source.at[slot], holder(up, part).at[n], block_sem.at[n, up, part]
                        ).start()
        for m in range(level):
            panel_copy(n, m).start()

    for n in range(npr):
        for up in range(level):
            size = sizes[up, chains[n][up]]
            for part, choices in enumerate(sources[up]):
                held = holder(up, part)
                pltpu.make_async_copy(choices[0].at[0], held.at[n], block_sem.at[n, up, part]).wait()
                count = (held.shape[1] - TAIL) // rows
                whole = product(held[n, count * rows :])
                for b in range(count):
                    value = held[n, b * rows : (b + 1) * rows] * whole
                    if up > 0 and part == 0:
                        l, m = b, up
                        value = jnp.where(live_lanes(value.shape, size), value, 0.0)
                    else:
                        l, m = up, b
                        value = jnp.where(
                            live_lanes(value.shape, sizes[m, chains[n][m]]), value, 0.0
                        )
                    top = value.astype(BF16)
                    split[n, m, l * rows : (l + 1) * rows] = top
                    split[n, m, high + l * rows : high + (l + 1) * rows] = (
                        value - top.astype(F32)
                    ).astype(BF16)

    results = []
    for n in range(npr):
        total = None
        for m in range(level):
            panel_copy(n, m).wait()
            block = lower[n, m].reshape(width, width)
            term = jnp.dot(split[n, m], block, preferred_element_type=F32)
            total = term if total is None else total + term
        value = -(total[:high] + total[high:])
        value = jnp.where(live_lanes(value.shape, sizes[level, row * npr + n]), value, 0.0)
        for l in range(level):
            cross[l, n] = value[l * rows : (l + 1) * rows]
        table, whole = factors(peak_of(value))
        value = value * (TOP / whole)
        if not last:
            passed[n, :high] = value
            passed[n, high:] = table
        results.append((value, table))
    for c in range(n_col):
        piece = slice(c * rows, (c + 1) * rows)
        turn[c, :high] = jnp.concatenate([v[:, piece] for v, _ in results], axis=1)
        turn[c, high:] = jnp.concatenate([t[:, piece] for _, t in results], axis=1)


def marginal_kernel(level, last, n_row, npr, rows, width, *refs):
    place, sizes, panel, turned, diag = refs[:5]
    n_out = 1 if last else 2
    at = 5
    outs = refs[at : at + n_out]
    lower, panel_sem = refs[at + n_out :]
    marginal = outs[0]
    message = None if last else outs[1]
    row, col = place[0], place[1]
    n_col = panel.shape[0]
    high = level * rows

    def panel_copy(n, m):
        return pltpu.make_async_copy(panel.at[:, m, n], lower.at[n, m], panel_sem.at[n, m])

    for m in range(level):
        for n in range(npr):
            panel_copy(n, m).start()

    scales = jnp.concatenate(
        [jnp.broadcast_to(product(turned[c, high:]), (rows, npr * rows)) for c in range(n_col)], axis=0
    )
    totals = [None] * npr
    sides = [[] for _ in range(npr)]
    for l in range(level):
        upright = turned[:, l * rows : (l + 1) * rows].reshape(width, npr * rows) * scales
        flat = upright.T
        top = flat.astype(BF16)
        low = (flat - top.astype(F32)).astype(BF16)
        for n in range(npr):
            mine = slice(n * rows, (n + 1) * rows)
            panel_copy(n, l).wait()
            block = lower[n, l].reshape(width, width)
            pair = jnp.concatenate([top[mine], low[mine]], axis=0)
            term = jnp.dot(pair, block, preferred_element_type=F32)
            term = term[:rows] + term[rows:]
            totals[n] = term if totals[n] is None else totals[n] + term
            sides[n].append(flat[mine])
    for n in range(npr):
        size = sizes[level, row * npr + n]
        value = diag_base(diag[n], size, col * rows, rows, width)
        value = value - jnp.where(live_lanes(value.shape, size), totals[n], 0.0)
        marginal[n] = value
        if not last:
            peak = peak_of(value)
            for side in sides[n]:
                peak = jnp.maximum(peak, peak_of(side))
            table, whole = factors(peak)
            scale = TOP / whole
            for l in range(level):
                message[n, l * rows : (l + 1) * rows] = sides[n][l] * scale
            message[n, high : high + rows] = value * scale
            message[n, high + rows :] = table


def params(limit=60 * 2**20):
    return pltpu.CompilerParams(vmem_limit_bytes=limit)


def shards(panel, diag_inverse, parents, supernode_sizes):
    levels, npr, rows, width = diag_inverse.shape
    n_row = lax.axis_size("row")
    n_col = lax.axis_size("col")
    place = jnp.stack([lax.axis_index("row"), lax.axis_index("col")]).astype(jnp.int32)

    def shape(*dims, dtype=F32):
        return jax.ShapeDtypeStruct(dims, dtype)

    def reach(level):
        return min(levels - 1 - level, n_row - 1)

    due = [[] for _ in range(levels)]

    def spread(message, level, at_once):
        found = [message]
        half = message.astype(F16)
        for back in range(1, reach(level) + 1):
            route = [(i, (i + back) % n_row) for i in range(n_row)]
            got = lax.ppermute(half, "row", route)
            when = level + back - 1
            if at_once or back > 1:
                due[min(when, levels - 1)].append(got)
            found.append(got.astype(F32))
        return found

    whole_panel = []
    for level in range(1, levels):
        start = level * (level - 1) // 2
        whole_panel.append(lax.all_gather(panel[start : start + level], "col", axis=0))

    base, message = pl.pallas_call(
        functools.partial(base_kernel, npr, rows, width),
        out_shape=(shape(npr, rows, width), shape(npr, rows + TAIL, width)),
        in_specs=[SMEM, SMEM, VMEM],
        out_specs=(VMEM, VMEM),
        compiler_params=params(),
        name="base",
    )(place, supernode_sizes, diag_inverse[0])
    crosses = []
    diagonals = [base]
    table = [[spread(message, 0, False)]]
    for level in range(1, levels):
        last = level == levels - 1
        high = level * rows
        whole = whole_panel[level - 1]
        spans = [min(level - up, n_row - 1) + 1 for up in range(level)]
        sources = [a for up in range(level) for part in table[up] for a in part[: spans[up]]]
        out_shape = [shape(level, npr, rows, width), shape(n_col, high + TAIL, npr * rows)]
        if not last:
            out_shape.append(shape(npr, high + TAIL, width))
        scratch = [
            pltpu.VMEM((npr, level, n_col, rows, width), BF16),
            pltpu.VMEM((npr, level, 2 * high, width), BF16),
            pltpu.SemaphoreType.DMA((npr, level)),
            pltpu.SemaphoreType.DMA((npr, level, 2)),
            pltpu.VMEM((npr, rows + TAIL, width), F32),
        ]
        for up in range(1, level):
            scratch.append(pltpu.VMEM((npr, up * rows + TAIL, width), F32))
            scratch.append(pltpu.VMEM((npr, (up + 1) * rows + TAIL, width), F32))
        made = pl.pallas_call(
            functools.partial(cross_kernel, level, last, spans, n_row, npr, rows, width),
            out_shape=tuple(out_shape),
            in_specs=[SMEM, SMEM, SMEM] + [ANY] * (1 + len(sources)),
            out_specs=(VMEM,) * len(out_shape),
            scratch_shapes=scratch,
            compiler_params=params(),
            name=f"cross{level}",
        )(place, parents, supernode_sizes, whole, *sources)
        crosses.append(made[0])
        ahead = None if last else spread(made[2], level, True)
        turned = lax.all_to_all(made[1].astype(F16), "col", 0, 0, tiled=True).astype(F32)
        for got in [] if last else due[level]:
            turned = jnp.where(got[0, -1, 0] > 0, turned, 0.0)
        out_shape = [shape(npr, rows, width)]
        if not last:
            out_shape.append(shape(npr, high + rows + TAIL, width))
        done = pl.pallas_call(
            functools.partial(marginal_kernel, level, last, n_row, npr, rows, width),
            out_shape=tuple(out_shape),
            in_specs=[SMEM, SMEM, ANY, VMEM, VMEM],
            out_specs=(VMEM,) * len(out_shape),
            scratch_shapes=[
                pltpu.VMEM((npr, level, n_col, rows, width), BF16),
                pltpu.SemaphoreType.DMA((npr, level)),
            ],
            compiler_params=params(),
            name=f"marginal{level}",
        )(place, supernode_sizes, whole, turned, diag_inverse[level])
        diagonals.append(done[0])
        if not last:
            table.append([ahead, spread(done[1], level, False)])
    return (jnp.concatenate(crosses, axis=0), jnp.stack(diagonals))


def solution(mesh):
    in_specs = (P(None, "row", "col", None), P(None, "row", "col", None), P(), P())
    out_specs = (P(None, "row", "col", None), P(None, "row", "col", None))
    return jax.shard_map(shards, mesh=mesh, in_specs=in_specs, out_specs=out_specs, check_vma=False)
```

```python
import functools

import jax
import jax.numpy as jnp
from jax import lax
from jax.experimental import pallas as pl
from jax.experimental.pallas import tpu as pltpu
from jax.sharding import PartitionSpec as P

F32 = jnp.float32
BF16 = jnp.bfloat16
F16 = jnp.float16
TOP = 2.0**14
TAIL = 8
VMEM = pl.BlockSpec(memory_space=pltpu.VMEM)
SMEM = pl.BlockSpec(memory_space=pltpu.SMEM)
ANY = pl.BlockSpec(memory_space=pl.ANY)


def factors(peak):
    rows = lax.broadcasted_iota(jnp.int32, (TAIL, peak.shape[1]), 0)
    rest = jnp.maximum(peak, 2.0**-100)
    table = jnp.ones((TAIL, peak.shape[1]), F32)
    whole = jnp.ones_like(rest)
    for i in range(TAIL):
        one = jnp.clip(rest, 2.0**-14, TOP).astype(BF16).astype(F32)
        rest = rest / one
        table = jnp.where(rows == i, jnp.broadcast_to(one, table.shape), table)
        whole = whole * one
    return table, whole


def product(table):
    whole = table[0:1]
    for i in range(1, TAIL):
        whole = whole * table[i : i + 1]
    return whole * (1.0 / TOP)


def peak_of(x):
    down = jnp.max(jnp.abs(x), axis=0, keepdims=True)
    return jnp.broadcast_to(jnp.max(down, axis=1, keepdims=True), down.shape)


def chain_of(parents, level, node):
    found = [None] * level
    for up in range(level - 1, -1, -1):
        node = parents[up, node]
        found[up] = node
    return found


def live_lanes(shape, size):
    return lax.broadcasted_iota(jnp.int32, shape, len(shape) - 1) < size


def base_kernel(npr, rows, width, place, sizes, diag, marginal, message):
    row, col = place[0], place[1]
    for n in range(npr):
        value = diag_base(diag[n], sizes[0, row * npr + n], col * rows, rows, width)
        marginal[n] = value
        table, whole = factors(peak_of(value))
        message[n, :rows] = value * (TOP / whole)
        message[n, rows:] = table


def diag_base(block, size, first, rows, width):
    lines = lax.broadcasted_iota(jnp.int32, (rows, width), 0) + first
    lanes = lax.broadcasted_iota(jnp.int32, (rows, width), 1)
    kept = jnp.where((lines < size) & (lanes < size), block, 0.0)
    return kept + jnp.where((lines == lanes) & (lines >= size), 1.0, 0.0)


def split_block(value, size, split, top_rows, low_rows):
    value = jnp.where(live_lanes(value.shape, size), value, 0.0)
    top = value.astype(BF16)
    split[top_rows] = top
    split[low_rows] = (value - top.astype(F32)).astype(BF16)


def upper_kernel(level, off, spans, n_row, npr, rows, width, *refs):
    place, parents, sizes, panel = refs[:4]
    at = 4
    sources = []
    for up in range(level):
        parts = []
        for part in range(2):
            if (up, part) == (0, 0) or (up, part) == (level - 1, 1):
                parts.append(())
                continue
            parts.append(refs[at : at + spans[up]])
            at += spans[up]
        sources.append(parts)
    out = refs[at]
    lower, split, panel_sem, block_sem = refs[at + 1 : at + 5]
    holders = iter(refs[at + 5 :])
    row = place[0]
    high = (level - 1) * rows
    held = {
        (up, part): next(holders)
        for up in range(level)
        for part in range(2)
        if sources[up][part]
    }
    chains = [chain_of(parents, level, row * npr + n) for n in range(npr)]

    def panel_copy(n, m):
        return pltpu.make_async_copy(panel.at[:, off + m, n], lower.at[n, m], panel_sem.at[n, m])

    for n in range(npr):
        for up in range(level):
            node = chains[n][up]
            back = lax.rem(row - lax.div(node, npr) + n_row, n_row)
            slot = lax.rem(node, npr)
            for part in range(2):
                for i, source in enumerate(sources[up][part]):

                    @pl.when(back == i)
                    def _():
                        pltpu.make_async_copy(
                            source.at[slot], held[up, part].at[n], block_sem.at[n, up, part]
                        ).start()
        for m in range(level):
            panel_copy(n, m).start()

    for n in range(npr):
        live = [sizes[up, chains[n][up]] for up in range(level)]
        total = None
        for up in range(level):
            for part in range(2):
                if not sources[up][part]:
                    continue
                block = held[up, part]
                pltpu.make_async_copy(
                    sources[up][part][0].at[0], block.at[n], block_sem.at[n, up, part]
                ).wait()
                count = (block.shape[1] - TAIL) // rows
                whole = product(block[n, count * rows :])
                for b in range(count):
                    value = block[n, b * rows : (b + 1) * rows] * whole
                    l, m = (b, up) if up > 0 and part == 0 else (up, b)
                    split_block(
                        value,
                        live[m],
                        split,
                        (n, m, slice(l * rows, (l + 1) * rows)),
                        (n, m, slice(high + l * rows, high + (l + 1) * rows)),
                    )
        for m in range(level):
            panel_copy(n, m).wait()
            block = lower[n, m].reshape(width, width)
            term = jnp.dot(split[n, m], block, preferred_element_type=F32)
            total = term if total is None else total + term
        value = -(total[:high] + total[high:])
        out[n] = jnp.where(live_lanes(value.shape, sizes[level, row * npr + n]), value, 0.0)


def cross_kernel(level, last, off, n_source, n_wait, n_row, npr, rows, width, *refs):
    place, parents, sizes, panel = refs[:4]
    sources = refs[4 : 4 + n_source]
    at = 4 + n_source
    upper = None
    if level > 1:
        upper = refs[at]
        at += 1
    at += n_wait
    n_out = 2 if last else 3
    outs = refs[at : at + n_out]
    lower, split, held, panel_sem, block_sem = refs[at + n_out :]
    cross, turn = outs[0], outs[1]
    passed = None if last else outs[2]
    row = place[0]
    n_col = panel.shape[0]
    high = level * rows
    chains = [chain_of(parents, level, row * npr + n) for n in range(npr)]

    def panel_copy(n, m):
        return pltpu.make_async_copy(panel.at[:, off + m, n], lower.at[n, m], panel_sem.at[n, m])

    for n in range(npr):
        node = chains[n][level - 1]
        back = lax.rem(row - lax.div(node, npr) + n_row, n_row)
        for i, source in enumerate(sources):

            @pl.when(back == i)
            def _():
                pltpu.make_async_copy(
                    source.at[lax.rem(node, npr)], held.at[n], block_sem.at[n]
                ).start()

    for m in range(level):
        for n in range(npr):
            panel_copy(n, m).start()

    for n in range(npr):
        pltpu.make_async_copy(sources[0].at[0], held.at[n], block_sem.at[n]).wait()
        whole = product(held[n, high:])
        for m in range(level):
            split_block(
                held[n, m * rows : (m + 1) * rows] * whole,
                sizes[m, chains[n][m]],
                split,
                (n, m, slice(0, rows)),
                (n, m, slice(rows, 2 * rows)),
            )
    totals = [None] * npr
    for m in range(level):
        for n in range(npr):
            panel_copy(n, m).wait()
            block = lower[n, m].reshape(width, width)
            term = jnp.dot(split[n, m], block, preferred_element_type=F32)
            totals[n] = term if totals[n] is None else totals[n] + term
    results = []
    for n in range(npr):
        value = -(totals[n][:rows] + totals[n][rows:])
        value = jnp.where(live_lanes(value.shape, sizes[level, row * npr + n]), value, 0.0)
        cross[level - 1, n] = value
        if level > 1:
            value = jnp.concatenate([upper[n], value], axis=0)
            for l in range(level - 1):
                cross[l, n] = value[l * rows : (l + 1) * rows]
        table, whole = factors(peak_of(value))
        value = value * (TOP / whole)
        if not last:
            passed[n, :high] = value
            passed[n, high:] = table
        results.append((value, table))
    for c in range(n_col):
        piece = slice(c * rows, (c + 1) * rows)
        turn[c, :high] = jnp.concatenate([v[:, piece] for v, _ in results], axis=1)
        turn[c, high:] = jnp.concatenate([t[:, piece] for _, t in results], axis=1)


def marginal_kernel(level, last, off, n_wait, n_row, npr, rows, width, *refs):
    place, sizes, panel, turned, diag = refs[:5]
    n_out = 1 if last else 2
    at = 5 + n_wait
    outs = refs[at : at + n_out]
    lower, panel_sem = refs[at + n_out :]
    marginal = outs[0]
    message = None if last else outs[1]
    row, col = place[0], place[1]
    n_col = panel.shape[0]
    high = level * rows

    def panel_copy(n, m):
        return pltpu.make_async_copy(panel.at[:, off + m, n], lower.at[n, m], panel_sem.at[n, m])

    for m in range(level):
        for n in range(npr):
            panel_copy(n, m).start()

    scales = jnp.concatenate(
        [jnp.broadcast_to(product(turned[c, high:]), (rows, npr * rows)) for c in range(n_col)], axis=0
    )
    totals = [None] * npr
    sides = [[] for _ in range(npr)]
    for l in range(level):
        upright = turned[:, l * rows : (l + 1) * rows].reshape(width, npr * rows) * scales
        flat = upright.T
        top = flat.astype(BF16)
        low = (flat - top.astype(F32)).astype(BF16)
        for n in range(npr):
            mine = slice(n * rows, (n + 1) * rows)
            panel_copy(n, l).wait()
            block = lower[n, l].reshape(width, width)
            pair = jnp.concatenate([top[mine], low[mine]], axis=0)
            term = jnp.dot(pair, block, preferred_element_type=F32)
            term = term[:rows] + term[rows:]
            totals[n] = term if totals[n] is None else totals[n] + term
            sides[n].append(flat[mine])
    for n in range(npr):
        size = sizes[level, row * npr + n]
        value = diag_base(diag[n], size, col * rows, rows, width)
        value = value - jnp.where(live_lanes(value.shape, size), totals[n], 0.0)
        marginal[n] = value
        if not last:
            peak = peak_of(value)
            for side in sides[n]:
                peak = jnp.maximum(peak, peak_of(side))
            table, whole = factors(peak)
            scale = TOP / whole
            for l in range(level):
                message[n, l * rows : (l + 1) * rows] = sides[n][l] * scale
            message[n, high : high + rows] = value * scale
            message[n, high + rows :] = table


def params(limit=60 * 2**20):
    return pltpu.CompilerParams(vmem_limit_bytes=limit)


def shards(panel, diag_inverse, parents, supernode_sizes):
    levels, npr, rows, width = diag_inverse.shape
    n_row = lax.axis_size("row")
    n_col = lax.axis_size("col")
    place = jnp.stack([lax.axis_index("row"), lax.axis_index("col")]).astype(jnp.int32)

    def shape(*dims, dtype=F32):
        return jax.ShapeDtypeStruct(dims, dtype)

    def reach(level):
        return min(levels - 1 - level, n_row - 1)

    due = [[] for _ in range(levels)]

    def spread(message, level, rows_only):
        found = [message]
        half = message.astype(F16)
        for back in range(1, reach(level) + 1):
            route = [(i, (i + back) % n_row) for i in range(n_row)]
            found.append(lax.ppermute(half, "row", route).astype(F32))
            if rows_only:
                due[level if back < 3 or level < 2 else level + back - 2].append(found[-1])
            elif back > 1:
                due[level if level == 0 else level + 1 if level == 1 else level + back - 1].append(found[-1])
        return found

    def gathered(first, count):
        return lax.all_gather(panel[first : first + count], "col", axis=0)

    whole_panel = [None] * levels
    ones = [lax.all_gather(panel[0:1, n : n + 1], "col", axis=0) for n in range(npr)]
    whole_panel[1] = (jnp.concatenate(ones, axis=2), 0)
    groups = [(2, 3), (4,), (5,)] if levels == 6 else [(level,) for level in range(2, levels)]
    for group in groups:
        first = group[0] * (group[0] - 1) // 2
        both = gathered(first, sum(group))
        for level in group:
            whole_panel[level] = (both, level * (level - 1) // 2 - first)

    base, message = pl.pallas_call(
        functools.partial(base_kernel, npr, rows, width),
        out_shape=(shape(npr, rows, width), shape(npr, rows + TAIL, width)),
        in_specs=[SMEM, SMEM, VMEM],
        out_specs=(VMEM, VMEM),
        compiler_params=params(),
        name="base",
    )(place, supernode_sizes, diag_inverse[0])
    crosses = []
    diagonals = [base]
    table = [[(), spread(message, 0, False)]]
    for level in range(1, levels):
        last = level == levels - 1
        high = level * rows
        whole, off = whole_panel[level]
        panel_scratch = [pltpu.VMEM((npr, level, n_col, rows, width), BF16)]
        upper = []
        if level > 1:
            spans = [min(level - up, n_row - 1) + 1 for up in range(level)]
            sources = []
            held = []
            for up in range(level):
                for part in range(2):
                    if (up, part) == (0, 0) or (up, part) == (level - 1, 1):
                        continue
                    sources.extend(table[up][part][: spans[up]])
                    held.append(pltpu.VMEM(table[up][part][0].shape, F32))
            upper = [
                pl.pallas_call(
                    functools.partial(upper_kernel, level, off, spans, n_row, npr, rows, width),
                    out_shape=shape(npr, high - rows, width),
                    in_specs=[SMEM, SMEM, SMEM] + [ANY] * (1 + len(sources)),
                    out_specs=VMEM,
                    scratch_shapes=panel_scratch
                    + [
                        pltpu.VMEM((npr, level, 2 * (high - rows), width), BF16),
                        pltpu.SemaphoreType.DMA((npr, level)),
                        pltpu.SemaphoreType.DMA((npr, level, 2)),
                    ]
                    + held,
                    compiler_params=params(),
                    name=f"upper{level}",
                )(place, parents, supernode_sizes, whole, *sources)
            ]
        newest = table[level - 1][1][: min(1, n_row - 1) + 1]
        waits = due[0] if level == 1 else []
        out_shape = [shape(level, npr, rows, width), shape(n_col, high + TAIL, npr * rows)]
        if not last:
            out_shape.append(shape(npr, high + TAIL, width))
        made = pl.pallas_call(
            functools.partial(
                cross_kernel, level, last, off, len(newest), len(waits), n_row, npr, rows, width
            ),
            out_shape=tuple(out_shape),
            in_specs=[SMEM, SMEM, SMEM] + [ANY] * (1 + len(newest)) + [VMEM] * len(upper) + [ANY] * len(waits),
            out_specs=(VMEM,) * len(out_shape),
            scratch_shapes=panel_scratch
            + [
                pltpu.VMEM((npr, level, 2 * rows, width), BF16),
                pltpu.VMEM((npr, high + TAIL, width), F32),
                pltpu.SemaphoreType.DMA((npr, level)),
                pltpu.SemaphoreType.DMA((npr,)),
            ],
            compiler_params=params(),
            name=f"cross{level}",
        )(place, parents, supernode_sizes, whole, *newest, *upper, *waits)
        crosses.append(made[0])
        ahead = () if last else spread(made[2], level, True)
        turned = lax.all_to_all(made[1].astype(F16), "col", 0, 0, tiled=True).astype(F32)
        waits = [] if last else due[level]
        out_shape = [shape(npr, rows, width)]
        if not last:
            out_shape.append(shape(npr, high + rows + TAIL, width))
        done = pl.pallas_call(
            functools.partial(marginal_kernel, level, last, off, len(waits), n_row, npr, rows, width),
            out_shape=tuple(out_shape),
            in_specs=[SMEM, SMEM, ANY, VMEM, VMEM] + [ANY] * len(waits),
            out_specs=(VMEM,) * len(out_shape),
            scratch_shapes=panel_scratch + [pltpu.SemaphoreType.DMA((npr, level))],
            compiler_params=params(),
            name=f"marginal{level}",
        )(place, supernode_sizes, whole, turned, diag_inverse[level], *waits)
        diagonals.append(done[0])
        if not last:
            table.append([ahead, spread(done[1], level, False)])
    return (jnp.concatenate(crosses, axis=0), jnp.stack(diagonals))


def solution(mesh):
    in_specs = (P(None, "row", "col", None), P(None, "row", "col", None), P(), P())
    out_specs = (P(None, "row", "col", None), P(None, "row", "col", None))
    return jax.shard_map(shards, mesh=mesh, in_specs=in_specs, out_specs=out_specs, check_vma=False)
```

```python
import functools

import jax
import jax.numpy as jnp
from jax import lax
from jax.experimental import pallas as pl
from jax.experimental.pallas import tpu as pltpu
from jax.sharding import PartitionSpec as P

F32 = jnp.float32
BF16 = jnp.bfloat16
F16 = jnp.float16
TOP = 2.0**14
TAIL = 8
VMEM = pl.BlockSpec(memory_space=pltpu.VMEM)
SMEM = pl.BlockSpec(memory_space=pltpu.SMEM)
ANY = pl.BlockSpec(memory_space=pl.ANY)


def factors(peak):
    rows = lax.broadcasted_iota(jnp.int32, (TAIL, peak.shape[1]), 0)
    rest = jnp.maximum(peak, 2.0**-100)
    table = jnp.ones((TAIL, peak.shape[1]), F32)
    whole = jnp.ones_like(rest)
    for i in range(TAIL):
        one = jnp.clip(rest, 2.0**-14, TOP).astype(BF16).astype(F32)
        rest = rest / one
        table = jnp.where(rows == i, jnp.broadcast_to(one, table.shape), table)
        whole = whole * one
    return table, whole


def product(table):
    whole = table[0:1]
    for i in range(1, TAIL):
        whole = whole * table[i : i + 1]
    return whole * (1.0 / TOP)


def peak_of(x):
    down = jnp.max(jnp.abs(x), axis=0, keepdims=True)
    return jnp.broadcast_to(jnp.max(down, axis=1, keepdims=True), down.shape)


def chain_of(parents, level, node):
    found = [None] * level
    for up in range(level - 1, -1, -1):
        node = parents[up, node]
        found[up] = node
    return found


def live_lanes(shape, size):
    return lax.broadcasted_iota(jnp.int32, shape, len(shape) - 1) < size


def base_kernel(npr, rows, width, place, sizes, diag, marginal, message):
    row, col = place[0], place[1]
    for n in range(npr):
        value = diag_base(diag[n], sizes[0, row * npr + n], col * rows, rows, width)
        marginal[n] = value
        table, whole = factors(peak_of(value))
        message[n, :rows] = value * (TOP / whole)
        message[n, rows:] = table


def diag_base(block, size, first, rows, width):
    lines = lax.broadcasted_iota(jnp.int32, (rows, width), 0) + first
    lanes = lax.broadcasted_iota(jnp.int32, (rows, width), 1)
    kept = jnp.where((lines < size) & (lanes < size), block, 0.0)
    return kept + jnp.where((lines == lanes) & (lines >= size), 1.0, 0.0)


def split_block(value, size, split, top_rows, low_rows):
    value = jnp.where(live_lanes(value.shape, size), value, 0.0)
    top = value.astype(BF16)
    split[top_rows] = top
    split[low_rows] = (value - top.astype(F32)).astype(BF16)


def upper_kernel(level, off, spans, n_row, npr, rows, width, *refs):
    place, parents, sizes, panel = refs[:4]
    at = 4
    sources = []
    for up in range(level):
        parts = []
        for part in range(2):
            if (up, part) == (0, 0) or (up, part) == (level - 1, 1):
                parts.append(())
                continue
            parts.append(refs[at : at + spans[up]])
            at += spans[up]
        sources.append(parts)
    out = refs[at]
    lower, split, panel_sem, block_sem = refs[at + 1 : at + 5]
    holders = iter(refs[at + 5 :])
    row = place[0]
    high = (level - 1) * rows
    held = {
        (up, part): next(holders)
        for up in range(level)
        for part in range(2)
        if sources[up][part]
    }
    chains = [chain_of(parents, level, row * npr + n) for n in range(npr)]

    def panel_copy(n, m):
        return pltpu.make_async_copy(panel.at[:, off + m, n], lower.at[n, m], panel_sem.at[n, m])

    for n in range(npr):
        for up in range(level):
            node = chains[n][up]
            back = lax.rem(row - lax.div(node, npr) + n_row, n_row)
            slot = lax.rem(node, npr)
            for part in range(2):
                for i, source in enumerate(sources[up][part]):

                    @pl.when(back == i)
                    def _():
                        pltpu.make_async_copy(
                            source.at[slot], held[up, part].at[n], block_sem.at[n, up, part]
                        ).start()
        for m in range(level):
            panel_copy(n, m).start()

    for n in range(npr):
        live = [sizes[up, chains[n][up]] for up in range(level)]
        total = None
        for up in range(level):
            for part in range(2):
                if not sources[up][part]:
                    continue
                block = held[up, part]
                pltpu.make_async_copy(
                    sources[up][part][0].at[0], block.at[n], block_sem.at[n, up, part]
                ).wait()
                count = (block.shape[1] - TAIL) // rows
                whole = product(block[n, count * rows :])
                for b in range(count):
                    value = block[n, b * rows : (b + 1) * rows] * whole
                    l, m = (b, up) if up > 0 and part == 0 else (up, b)
                    split_block(
                        value,
                        live[m],
                        split,
                        (n, m, slice(l * rows, (l + 1) * rows)),
                        (n, m, slice(high + l * rows, high + (l + 1) * rows)),
                    )
        for m in range(level):
            panel_copy(n, m).wait()
            block = lower[n, m].reshape(width, width)
            term = jnp.dot(split[n, m], block, preferred_element_type=F32)
            total = term if total is None else total + term
        value = -(total[:high] + total[high:])
        out[n] = jnp.where(live_lanes(value.shape, sizes[level, row * npr + n]), value, 0.0)


def cross_kernel(level, last, off, n_source, n_wait, n_row, npr, rows, width, *refs):
    place, parents, sizes, panel = refs[:4]
    sources = refs[4 : 4 + n_source]
    at = 4 + n_source
    upper = None
    if level > 1:
        upper = refs[at]
        at += 1
    at += n_wait
    n_out = 2 if last else 3
    outs = refs[at : at + n_out]
    lower, split, held, panel_sem, block_sem = refs[at + n_out :]
    cross, turn = outs[0], outs[1]
    passed = None if last else outs[2]
    row = place[0]
    n_col = panel.shape[0]
    high = level * rows
    chains = [chain_of(parents, level, row * npr + n) for n in range(npr)]

    def panel_copy(n, m):
        return pltpu.make_async_copy(panel.at[:, off + m, n], lower.at[n, m], panel_sem.at[n, m])

    for n in range(npr):
        node = chains[n][level - 1]
        back = lax.rem(row - lax.div(node, npr) + n_row, n_row)
        for i, source in enumerate(sources):

            @pl.when(back == i)
            def _():
                pltpu.make_async_copy(
                    source.at[lax.rem(node, npr)], held.at[n], block_sem.at[n]
                ).start()

    for m in range(level):
        for n in range(npr):
            panel_copy(n, m).start()

    for n in range(npr):
        pltpu.make_async_copy(sources[0].at[0], held.at[n], block_sem.at[n]).wait()
        whole = product(held[n, high:])
        for m in range(level):
            split_block(
                held[n, m * rows : (m + 1) * rows] * whole,
                sizes[m, chains[n][m]],
                split,
                (n, m, slice(0, rows)),
                (n, m, slice(rows, 2 * rows)),
            )
    totals = [None] * npr
    for m in range(level):
        for n in range(npr):
            panel_copy(n, m).wait()
            block = lower[n, m].reshape(width, width)
            term = jnp.dot(split[n, m], block, preferred_element_type=F32)
            totals[n] = term if totals[n] is None else totals[n] + term
    results = []
    for n in range(npr):
        value = -(totals[n][:rows] + totals[n][rows:])
        value = jnp.where(live_lanes(value.shape, sizes[level, row * npr + n]), value, 0.0)
        cross[level - 1, n] = value
        if level > 1:
            value = jnp.concatenate([upper[n], value], axis=0)
            for l in range(level - 1):
                cross[l, n] = value[l * rows : (l + 1) * rows]
        table, whole = factors(peak_of(value))
        value = value * (TOP / whole)
        if not last:
            passed[n, :high] = value
            passed[n, high:] = table
        results.append((value, table))
    for c in range(n_col):
        piece = slice(c * rows, (c + 1) * rows)
        turn[c, :high] = jnp.concatenate([v[:, piece] for v, _ in results], axis=1)
        turn[c, high:] = jnp.concatenate([t[:, piece] for _, t in results], axis=1)


def marginal_kernel(level, last, off, n_wait, n_row, npr, rows, width, *refs):
    place, sizes, panel, turned, diag = refs[:5]
    n_out = 1 if last else 2
    at = 5 + n_wait
    outs = refs[at : at + n_out]
    lower, panel_sem = refs[at + n_out :]
    marginal = outs[0]
    message = None if last else outs[1]
    row, col = place[0], place[1]
    n_col = panel.shape[0]
    high = level * rows

    def panel_copy(n, m):
        return pltpu.make_async_copy(panel.at[:, off + m, n], lower.at[n, m], panel_sem.at[n, m])

    for m in range(level):
        for n in range(npr):
            panel_copy(n, m).start()

    scales = jnp.concatenate(
        [jnp.broadcast_to(product(turned[c, high:]), (rows, npr * rows)) for c in range(n_col)], axis=0
    )
    totals = [None] * npr
    sides = [[] for _ in range(npr)]
    for l in range(level):
        upright = turned[:, l * rows : (l + 1) * rows].reshape(width, npr * rows) * scales
        flat = upright.T
        top = flat.astype(BF16)
        low = (flat - top.astype(F32)).astype(BF16)
        for n in range(npr):
            mine = slice(n * rows, (n + 1) * rows)
            panel_copy(n, l).wait()
            block = lower[n, l].reshape(width, width)
            pair = jnp.concatenate([top[mine], low[mine]], axis=0)
            term = jnp.dot(pair, block, preferred_element_type=F32)
            term = term[:rows] + term[rows:]
            totals[n] = term if totals[n] is None else totals[n] + term
            sides[n].append(flat[mine])
    for n in range(npr):
        size = sizes[level, row * npr + n]
        value = diag_base(diag[n], size, col * rows, rows, width)
        value = value - jnp.where(live_lanes(value.shape, size), totals[n], 0.0)
        marginal[n] = value
        if not last:
            peak = peak_of(value)
            for side in sides[n]:
                peak = jnp.maximum(peak, peak_of(side))
            table, whole = factors(peak)
            scale = TOP / whole
            for l in range(level):
                message[n, l * rows : (l + 1) * rows] = sides[n][l] * scale
            message[n, high : high + rows] = value * scale
            message[n, high + rows :] = table


def params(limit=60 * 2**20):
    return pltpu.CompilerParams(vmem_limit_bytes=limit)


def shards(panel, diag_inverse, parents, supernode_sizes):
    levels, npr, rows, width = diag_inverse.shape
    n_row = lax.axis_size("row")
    n_col = lax.axis_size("col")
    place = jnp.stack([lax.axis_index("row"), lax.axis_index("col")]).astype(jnp.int32)

    def shape(*dims, dtype=F32):
        return jax.ShapeDtypeStruct(dims, dtype)

    def reach(level):
        return min(levels - 1 - level, n_row - 1)

    due = [[] for _ in range(levels)]

    def spread(message, level, rows_only):
        found = [message]
        half = message.astype(F16)
        for back in range(1, reach(level) + 1):
            route = [(i, (i + back) % n_row) for i in range(n_row)]
            found.append(lax.ppermute(half, "row", route).astype(F32))
            if rows_only:
                due[level if back < 3 or level < 2 else level + back - 2].append(found[-1])
            elif back > 1:
                due[level if level == 0 else level + 1 if level == 1 else level + back - 1].append(found[-1])
        return found

    def gathered(first, count):
        return lax.all_gather(panel[first : first + count], "col", axis=0)

    whole_panel = [None] * levels
    for group in [(level,) for level in range(1, levels)]:
        first = group[0] * (group[0] - 1) // 2
        both = gathered(first, sum(group))
        for level in group:
            whole_panel[level] = (both, level * (level - 1) // 2 - first)

    base, message = pl.pallas_call(
        functools.partial(base_kernel, npr, rows, width),
        out_shape=(shape(npr, rows, width), shape(npr, rows + TAIL, width)),
        in_specs=[SMEM, SMEM, VMEM],
        out_specs=(VMEM, VMEM),
        compiler_params=params(),
        name="base",
    )(place, supernode_sizes, diag_inverse[0])
    crosses = []
    diagonals = [base]
    table = [[(), spread(message, 0, False)]]
    for level in range(1, levels):
        last = level == levels - 1
        high = level * rows
        whole, off = whole_panel[level]
        panel_scratch = [pltpu.VMEM((npr, level, n_col, rows, width), BF16)]
        upper = []
        if level > 1:
            spans = [min(level - up, n_row - 1) + 1 for up in range(level)]
            sources = []
            held = []
            for up in range(level):
                for part in range(2):
                    if (up, part) == (0, 0) or (up, part) == (level - 1, 1):
                        continue
                    sources.extend(table[up][part][: spans[up]])
                    held.append(pltpu.VMEM(table[up][part][0].shape, F32))
            upper = [
                pl.pallas_call(
                    functools.partial(upper_kernel, level, off, spans, n_row, npr, rows, width),
                    out_shape=shape(npr, high - rows, width),
                    in_specs=[SMEM, SMEM, SMEM] + [ANY] * (1 + len(sources)),
                    out_specs=VMEM,
                    scratch_shapes=panel_scratch
                    + [
                        pltpu.VMEM((npr, level, 2 * (high - rows), width), BF16),
                        pltpu.SemaphoreType.DMA((npr, level)),
                        pltpu.SemaphoreType.DMA((npr, level, 2)),
                    ]
                    + held,
                    compiler_params=params(),
                    name=f"upper{level}",
                )(place, parents, supernode_sizes, whole, *sources)
            ]
        newest = table[level - 1][1][: min(1, n_row - 1) + 1]
        waits = due[0] if level == 1 else []
        out_shape = [shape(level, npr, rows, width), shape(n_col, high + TAIL, npr * rows)]
        if not last:
            out_shape.append(shape(npr, high + TAIL, width))
        made = pl.pallas_call(
            functools.partial(
                cross_kernel, level, last, off, len(newest), len(waits), n_row, npr, rows, width
            ),
            out_shape=tuple(out_shape),
            in_specs=[SMEM, SMEM, SMEM] + [ANY] * (1 + len(newest)) + [VMEM] * len(upper) + [ANY] * len(waits),
            out_specs=(VMEM,) * len(out_shape),
            scratch_shapes=panel_scratch
            + [
                pltpu.VMEM((npr, level, 2 * rows, width), BF16),
                pltpu.VMEM((npr, high + TAIL, width), F32),
                pltpu.SemaphoreType.DMA((npr, level)),
                pltpu.SemaphoreType.DMA((npr,)),
            ],
            compiler_params=params(),
            name=f"cross{level}",
        )(place, parents, supernode_sizes, whole, *newest, *upper, *waits)
        crosses.append(made[0])
        ahead = () if last else spread(made[2], level, True)
        turned = lax.all_to_all(made[1].astype(F16), "col", 0, 0, tiled=True).astype(F32)
        waits = [] if last else due[level] + ([whole_panel[level + 1][0]] if level > 1 else [])
        out_shape = [shape(npr, rows, width)]
        if not last:
            out_shape.append(shape(npr, high + rows + TAIL, width))
        done = pl.pallas_call(
            functools.partial(marginal_kernel, level, last, off, len(waits), n_row, npr, rows, width),
            out_shape=tuple(out_shape),
            in_specs=[SMEM, SMEM, ANY, VMEM, VMEM] + [ANY] * len(waits),
            out_specs=(VMEM,) * len(out_shape),
            scratch_shapes=panel_scratch + [pltpu.SemaphoreType.DMA((npr, level))],
            compiler_params=params(),
            name=f"marginal{level}",
        )(place, supernode_sizes, whole, turned, diag_inverse[level], *waits)
        diagonals.append(done[0])
        if not last:
            table.append([ahead, spread(done[1], level, False)])
    return (jnp.concatenate(crosses, axis=0), jnp.stack(diagonals))


def solution(mesh):
    in_specs = (P(None, "row", "col", None), P(None, "row", "col", None), P(), P())
    out_specs = (P(None, "row", "col", None), P(None, "row", "col", None))
    return jax.shard_map(shards, mesh=mesh, in_specs=in_specs, out_specs=out_specs, check_vma=False)
```

```python
import functools

import jax
import jax.numpy as jnp
from jax import lax
from jax.experimental import pallas as pl
from jax.experimental.pallas import tpu as pltpu
from jax.sharding import PartitionSpec as P

F32 = jnp.float32
BF16 = jnp.bfloat16
F16 = jnp.float16
TOP = 2.0**14
TAIL = 8
VMEM = pl.BlockSpec(memory_space=pltpu.VMEM)
SMEM = pl.BlockSpec(memory_space=pltpu.SMEM)
ANY = pl.BlockSpec(memory_space=pl.ANY)


def factors(peak):
    rows = lax.broadcasted_iota(jnp.int32, (TAIL, peak.shape[1]), 0)
    rest = jnp.maximum(peak, 2.0**-100)
    table = jnp.ones((TAIL, peak.shape[1]), F32)
    whole = jnp.ones_like(rest)
    for i in range(TAIL):
        one = jnp.clip(rest, 2.0**-14, TOP).astype(BF16).astype(F32)
        rest = rest / one
        table = jnp.where(rows == i, jnp.broadcast_to(one, table.shape), table)
        whole = whole * one
    return table, whole


def product(table):
    whole = table[0:1]
    for i in range(1, TAIL):
        whole = whole * table[i : i + 1]
    return whole * (1.0 / TOP)


def peak_of(x):
    down = jnp.max(jnp.abs(x), axis=0, keepdims=True)
    return jnp.broadcast_to(jnp.max(down, axis=1, keepdims=True), down.shape)


def chain_of(parents, level, node):
    found = [None] * level
    for up in range(level - 1, -1, -1):
        node = parents[up, node]
        found[up] = node
    return found


def live_lanes(shape, size):
    return lax.broadcasted_iota(jnp.int32, shape, len(shape) - 1) < size


def base_kernel(npr, rows, width, place, sizes, whole_diag, out, message, marginal, diag, out_sem):
    row, col = place[0], place[1]
    bring = pltpu.make_async_copy(whole_diag.at[0], diag, out_sem)
    bring.start()
    bring.wait()
    for n in range(npr):
        value = diag_base(diag[n], sizes[0, row * npr + n], col * rows, rows, width)
        marginal[n] = value
        table, whole = factors(peak_of(value))
        message[n, :rows] = value * (TOP / whole)
        message[n, rows:] = table
    keep = pltpu.make_async_copy(marginal, out.at[0], out_sem)
    keep.start()
    keep.wait()


def diag_base(block, size, first, rows, width):
    lines = lax.broadcasted_iota(jnp.int32, (rows, width), 0) + first
    lanes = lax.broadcasted_iota(jnp.int32, (rows, width), 1)
    kept = jnp.where((lines < size) & (lanes < size), block, 0.0)
    return kept + jnp.where((lines == lanes) & (lines >= size), 1.0, 0.0)


def pack(turn, values, rows):
    high = values[0].shape[0]
    parts = []
    for value in values:
        table, whole = factors(peak_of(value))
        parts.append((value * (TOP / whole), table))
    for c in range(turn.shape[0]):
        piece = slice(c * rows, (c + 1) * rows)
        turn[c, :high] = jnp.concatenate([v[:, piece] for v, _ in parts], axis=1)
        turn[c, high:] = jnp.concatenate([t[:, piece] for _, t in parts], axis=1)


def panel_moves(panel, off, lower, sem, col, n_col):
    def start(n, m):
        if len(panel) == 1:
            pltpu.make_async_copy(panel[0].at[:, off + m, n], lower.at[n, m], sem.at[n, m]).start()
            return
        z, core = lax.div(col, 2), lax.rem(col, 2)
        for i, piece in enumerate(panel):
            owner = lax.rem(z - i // 2 + n_col // 2, n_col // 2) * 2 + (core if i % 2 == 0 else 1 - core)
            pltpu.make_async_copy(piece.at[m, n], lower.at[n, m, owner], sem.at[n, m]).start()

    def wait(n, m):
        pltpu.make_async_copy(lower.at[n, m], lower.at[n, m], sem.at[n, m]).wait()

    return start, wait


def split_block(value, size, split, top_rows, low_rows):
    value = jnp.where(live_lanes(value.shape, size), value, 0.0)
    top = value.astype(BF16)
    split[top_rows] = top
    split[low_rows] = (value - top.astype(F32)).astype(BF16)


def upper_kernel(level, n_panel, off, n_wait, spans, n_row, npr, rows, width, *refs):
    place, parents, sizes = refs[:3]
    panel = refs[3 : 3 + n_panel]
    at = 3 + n_panel
    sources = []
    for up in range(level):
        parts = []
        for part in range(2):
            if (up, part) == (0, 0) or (up, part) == (level - 1, 1):
                parts.append(())
                continue
            parts.append(refs[at : at + spans[up]])
            at += spans[up]
        sources.append(parts)
    at += n_wait
    out, turn = refs[at : at + 2]
    lower, split, panel_sem, block_sem = refs[at + 2 : at + 6]
    holders = iter(refs[at + 6 :])
    row = place[0]
    high = (level - 1) * rows
    held = {
        (up, part): next(holders)
        for up in range(level)
        for part in range(2)
        if sources[up][part]
    }
    chains = [chain_of(parents, level, row * npr + n) for n in range(npr)]

    start, wait = panel_moves(panel, off, lower, panel_sem, place[1], lower.shape[2])

    for n in range(npr):
        for up in range(level):
            node = chains[n][up]
            back = lax.rem(row - lax.div(node, npr) + n_row, n_row)
            slot = lax.rem(node, npr)
            for part in range(2):
                for i, source in enumerate(sources[up][part]):

                    @pl.when(back == i)
                    def _():
                        pltpu.make_async_copy(
                            source.at[slot], held[up, part].at[n], block_sem.at[n, up, part]
                        ).start()
        for m in range(level):
            start(n, m)

    values = []
    for n in range(npr):
        live = [sizes[up, chains[n][up]] for up in range(level)]
        total = None
        for up in range(level):
            for part in range(2):
                if not sources[up][part]:
                    continue
                block = held[up, part]
                pltpu.make_async_copy(
                    sources[up][part][0].at[0], block.at[n], block_sem.at[n, up, part]
                ).wait()
                count = (block.shape[1] - TAIL) // rows
                whole = product(block[n, count * rows :])
                for b in range(count):
                    value = block[n, b * rows : (b + 1) * rows] * whole
                    l, m = (b, up) if up > 0 and part == 0 else (up, b)
                    split_block(
                        value,
                        live[m],
                        split,
                        (n, m, slice(l * rows, (l + 1) * rows)),
                        (n, m, slice(high + l * rows, high + (l + 1) * rows)),
                    )
        for m in range(level):
            wait(n, m)
            block = lower[n, m].reshape(width, width)
            term = jnp.dot(split[n, m], block, preferred_element_type=F32)
            total = term if total is None else total + term
        value = -(total[:high] + total[high:])
        values.append(jnp.where(live_lanes(value.shape, sizes[level, row * npr + n]), value, 0.0))
        out[n] = values[n]
    pack(turn, values, rows)


def cross_kernel(level, last, n_panel, off, n_source, n_wait, n_row, npr, rows, width, *refs):
    place, parents, sizes = refs[:3]
    panel = refs[3 : 3 + n_panel]
    sources = refs[3 + n_panel : 3 + n_panel + n_source]
    at = 3 + n_panel + n_source
    upper = None
    if level > 1:
        upper = refs[at]
        at += 1
    at += n_wait
    n_out = 2 if last else 3
    outs = refs[at : at + n_out]
    lower, split, held, panel_sem, block_sem, cross, out_sem = refs[at + n_out :]
    out, turn = outs[0], outs[1]
    passed = None if last else outs[2]
    row = place[0]
    high = level * rows
    chains = [chain_of(parents, level, row * npr + n) for n in range(npr)]

    start, wait = panel_moves(panel, off, lower, panel_sem, place[1], lower.shape[2])

    for n in range(npr):
        node = chains[n][level - 1]
        back = lax.rem(row - lax.div(node, npr) + n_row, n_row)
        for i, source in enumerate(sources):

            @pl.when(back == i)
            def _():
                pltpu.make_async_copy(
                    source.at[lax.rem(node, npr)], held.at[n], block_sem.at[n]
                ).start()

    for m in range(level):
        for n in range(npr):
            start(n, m)

    for n in range(npr):
        pltpu.make_async_copy(sources[0].at[0], held.at[n], block_sem.at[n]).wait()
        whole = product(held[n, high:])
        for m in range(level):
            split_block(
                held[n, m * rows : (m + 1) * rows] * whole,
                sizes[m, chains[n][m]],
                split,
                (n, m, slice(0, rows)),
                (n, m, slice(rows, 2 * rows)),
            )
    totals = [None] * npr
    for m in range(level):
        for n in range(npr):
            wait(n, m)
            block = lower[n, m].reshape(width, width)
            term = jnp.dot(split[n, m], block, preferred_element_type=F32)
            totals[n] = term if totals[n] is None else totals[n] + term
    values = []
    for n in range(npr):
        value = -(totals[n][:rows] + totals[n][rows:])
        values.append(jnp.where(live_lanes(value.shape, sizes[level, row * npr + n]), value, 0.0))
    for n in range(npr):
        cross[level - 1, n] = values[n]
        for l in range(level - 1):
            cross[l, n] = upper[n, l * rows : (l + 1) * rows]
    first = level * (level - 1) // 2
    keep = pltpu.make_async_copy(cross, out.at[first : first + level], out_sem)
    keep.start()
    pack(turn, values, rows)
    for n in range(npr):
        value = values[n]
        if level > 1:
            value = jnp.concatenate([upper[n], value], axis=0)
        if not last:
            table, whole = factors(peak_of(value))
            passed[n, :high] = value * (TOP / whole)
            passed[n, high:] = table
    keep.wait()


def marginal_kernel(level, last, n_panel, off, n_wait, n_row, npr, rows, width, *refs):
    place, sizes, diag = refs[:3]
    n_turned = min(level, 2)
    turned = refs[3 : 3 + n_turned]
    panel = refs[3 + n_turned : 3 + n_turned + n_panel]
    n_out = 1 if last else 2
    at = 3 + n_turned + n_panel + n_wait
    outs = refs[at : at + n_out]
    lower, panel_sem, marginal, out_sem = refs[at + n_out :]
    message = None if last else outs[1]
    row, col = place[0], place[1]
    n_col = lower.shape[2]
    high = level * rows

    start, wait = panel_moves(panel, off, lower, panel_sem, place[1], lower.shape[2])

    for m in range(level):
        for n in range(npr):
            start(n, m)

    def scales_of(part):
        lines = part.shape[1] - TAIL
        return jnp.concatenate(
            [jnp.broadcast_to(product(part[c, lines:]), (rows, npr * rows)) for c in range(n_col)], axis=0
        )

    scales = [scales_of(part) for part in turned]
    totals = [None] * npr
    sides = [[] for _ in range(npr)]
    for l in range(level):
        i, at_row = (n_turned - 1, 0) if l == level - 1 else (0, l * rows)
        upright = turned[i][:, at_row : at_row + rows].reshape(width, npr * rows) * scales[i]
        flat = upright.T
        top = flat.astype(BF16)
        low = (flat - top.astype(F32)).astype(BF16)
        for n in range(npr):
            mine = slice(n * rows, (n + 1) * rows)
            wait(n, l)
            block = lower[n, l].reshape(width, width)
            pair = jnp.concatenate([top[mine], low[mine]], axis=0)
            term = jnp.dot(pair, block, preferred_element_type=F32)
            term = term[:rows] + term[rows:]
            totals[n] = term if totals[n] is None else totals[n] + term
            sides[n].append(flat[mine])
    for n in range(npr):
        size = sizes[level, row * npr + n]
        value = diag_base(diag[n], size, col * rows, rows, width)
        value = value - jnp.where(live_lanes(value.shape, size), totals[n], 0.0)
        marginal[n] = value
        if n == npr - 1:
            keep = pltpu.make_async_copy(marginal, outs[0].at[level], out_sem)
            keep.start()
        if not last:
            peak = peak_of(value)
            for side in sides[n]:
                peak = jnp.maximum(peak, peak_of(side))
            table, whole = factors(peak)
            scale = TOP / whole
            for l in range(level):
                message[n, l * rows : (l + 1) * rows] = sides[n][l] * scale
            message[n, high : high + rows] = value * scale
            message[n, high + rows :] = table
    keep.wait()


def gate_kernel(count, *refs):
    refs[count][...] = jnp.ones((1, 1, 1), F32)


def timing(rows_only, level, back):
    if level == 0 or (back == 1 and not rows_only):
        return ("due", level + 1) if back > 1 else ("free", -1)
    if rows_only:
        if back == 1:
            return "due", level
        return "due", (level if back < 3 or level < 2 else level + back - 2)
    return "due", (level + 1 if level == 1 else level + back - 1)


def params(limit=60 * 2**20):
    return pltpu.CompilerParams(vmem_limit_bytes=limit)


def shards(panel, diag_inverse, parents, supernode_sizes):
    levels, npr, rows, width = diag_inverse.shape
    n_row = lax.axis_size("row")
    n_col = lax.axis_size("col")
    place = jnp.stack([lax.axis_index("row"), lax.axis_index("col")]).astype(jnp.int32)

    def shape(*dims, dtype=F32):
        return jax.ShapeDtypeStruct(dims, dtype)

    def reach(level):
        return min(levels - 1 - level, n_row - 1)

    def gate(name, arrays):
        return pl.pallas_call(
            functools.partial(gate_kernel, len(arrays)),
            out_shape=shape(1, 1, 1),
            in_specs=[ANY] * len(arrays),
            out_specs=VMEM,
            name=name,
        )(*arrays)

    due = [[] for _ in range(levels)]
    gates = [[] for _ in range(levels)]

    def spread(message, level, rows_only):
        found = [message]
        half = message
        if rows_only and gates[level]:
            half = jnp.where(gate(f"gate{level}", gates[level]) > 0, message, 0.0)
        half = half.astype(F16)
        for back in range(1, reach(level) + 1):
            route = [(i, (i + back) % n_row) for i in range(n_row)]
            found.append(lax.ppermute(half, "row", route).astype(F32))
            where, when = timing(rows_only, level, back)
            {"due": due, "gate": gates, "free": due + [[]]}[where][when].append(found[-1])
        return found

    def turn_over(message):
        return lax.all_to_all(message.astype(F16), "col", 0, 0, tiled=True).astype(F32)

    def gathered(first, count, there):
        mine = jnp.where(there.astype(BF16).reshape(1, 1, 1, 1) > 0, panel[first : first + count], 0)
        return lax.all_gather(mine, "col", axis=0)

    def pieces(mine):
        swap = [(i, i ^ 1) for i in range(n_col)]
        found = []
        for back in range(n_col // 2):
            got = mine
            if back:
                got = lax.ppermute(mine, "col", [(i, (i + 2 * back) % n_col) for i in range(n_col)])
            found += [got, lax.ppermute(got, "col", swap)]
        return found

    whole_panel = [None] * levels
    whole_panel[1] = (pieces(panel[0:1]), 0)
    diagonals, message = pl.pallas_call(
        functools.partial(base_kernel, npr, rows, width),
        out_shape=(shape(levels, npr, rows, width), shape(npr, rows + TAIL, width)),
        in_specs=[SMEM, SMEM, ANY],
        out_specs=(ANY, VMEM),
        scratch_shapes=[
            pltpu.VMEM((npr, rows, width), F32),
            pltpu.VMEM((npr, rows, width), F32),
            pltpu.SemaphoreType.DMA(()),
        ],
        compiler_params=params(),
        name="base",
    )(place, supernode_sizes, diag_inverse)
    crosses = None
    table = [[(), spread(message, 0, False)]]

    def gather_level(level, there):
        first = level * (level - 1) // 2
        whole_panel[level] = ([gathered(first, level, there)], 0)

    there = gate("first", whole_panel[1][0][::2] + [message])
    for deeper in range(2, levels):
        gather_level(deeper, there)
    for level in range(1, levels):
        last = level == levels - 1
        high = level * rows
        whole, off = whole_panel[level]
        panel_scratch = [pltpu.VMEM((npr, level, n_col, rows, width), BF16)]
        upper = []
        turned = []
        if level > 1:
            spans = [min(level - up, n_row - 1) + 1 for up in range(level)]
            sources = []
            held = []
            for up in range(level):
                for part in range(2):
                    if (up, part) == (0, 0) or (up, part) == (level - 1, 1):
                        continue
                    sources.extend(table[up][part][: spans[up]])
                    held.append(pltpu.VMEM(table[up][part][0].shape, F32))
            upper = list(
                pl.pallas_call(
                    functools.partial(upper_kernel, level, len(whole), off, 1, spans, n_row, npr, rows, width),
                    out_shape=(
                        shape(npr, high - rows, width),
                        shape(n_col, high - rows + TAIL, npr * rows),
                    ),
                    in_specs=[SMEM, SMEM, SMEM] + [ANY] * (len(whole) + len(sources) + 1),
                    out_specs=(VMEM, VMEM),
                    scratch_shapes=panel_scratch
                    + [
                        pltpu.VMEM((npr, level, 2 * (high - rows), width), BF16),
                        pltpu.SemaphoreType.DMA((npr, level)),
                        pltpu.SemaphoreType.DMA((npr, level, 2)),
                    ]
                    + held,
                    compiler_params=params(),
                    name=f"upper{level}",
                )(place, parents, supernode_sizes, *whole, *sources, table[level - 1][1][0])
            )
            turned.append(turn_over(upper.pop()))
        newest = table[level - 1][1][: min(1, n_row - 1) + 1]
        waits = due[0] if level == 1 else []
        out_shape = [shape(panel.shape[0], npr, rows, width), shape(n_col, rows + TAIL, npr * rows)]
        if not last:
            out_shape.append(shape(npr, high + TAIL, width))
        before = [] if crosses is None else [crosses]
        n_given = 3 + len(whole) + len(newest) + len(upper) + len(waits)
        made = pl.pallas_call(
            functools.partial(
                cross_kernel, level, last, len(whole), off, len(newest), len(waits) + len(before), n_row, npr, rows, width
            ),
            out_shape=tuple(out_shape),
            in_specs=[SMEM, SMEM, SMEM] + [ANY] * (len(whole) + len(newest)) + [VMEM] * len(upper) + [ANY] * (len(waits) + len(before)),
            out_specs=(ANY,) + (VMEM,) * (len(out_shape) - 1),
            scratch_shapes=panel_scratch
            + [
                pltpu.VMEM((npr, level, 2 * rows, width), BF16),
                pltpu.VMEM((npr, high + TAIL, width), F32),
                pltpu.SemaphoreType.DMA((npr, level)),
                pltpu.SemaphoreType.DMA((npr,)),
                pltpu.VMEM((level, npr, rows, width), F32),
                pltpu.SemaphoreType.DMA(()),
            ],
            input_output_aliases={n_given: 0} if before else {},
            compiler_params=params(),
            cost_estimate=pl.CostEstimate(flops=4 * 10**10, bytes_accessed=2**20, transcendentals=0) if last else None,
            name=f"cross{level}",
        )(place, parents, supernode_sizes, *whole, *newest, *upper, *waits, *before)
        crosses = made[0]
        ahead = () if last else spread(made[2], level, True)
        newer = made[1]
        if last and turned:
            newer = jnp.where(gate(f"turn{level}", turned) > 0, newer, 0.0)
        turned.append(turn_over(newer))
        waits = [] if last else due[level] + whole_panel[level + 1][0]
        out_shape = [shape(levels, npr, rows, width)]
        if not last:
            out_shape.append(shape(npr, high + rows + TAIL, width))
        done = pl.pallas_call(
            functools.partial(marginal_kernel, level, last, len(whole), off, len(waits) + 1, n_row, npr, rows, width),
            out_shape=tuple(out_shape),
            in_specs=[SMEM, SMEM, VMEM] + [VMEM] * len(turned) + [ANY] * (len(whole) + len(waits) + 1),
            out_specs=(ANY,) + (VMEM,) * (len(out_shape) - 1),
            scratch_shapes=panel_scratch
            + [
                pltpu.SemaphoreType.DMA((npr, level)),
                pltpu.VMEM((npr, rows, width), F32),
                pltpu.SemaphoreType.DMA(()),
            ],
            input_output_aliases={3 + len(turned) + len(whole) + len(waits): 0},
            compiler_params=params(),
            name=f"marginal{level}",
        )(place, supernode_sizes, diag_inverse[level], *turned, *whole, *waits, diagonals)
        diagonals = done[0]
        if not last:
            table.append([ahead, spread(done[1], level, False)])
    return crosses, diagonals


def solution(mesh):
    in_specs = (P(None, "row", "col", None), P(None, "row", "col", None), P(), P())
    out_specs = (P(None, "row", "col", None), P(None, "row", "col", None))
    return jax.shard_map(shards, mesh=mesh, in_specs=in_specs, out_specs=out_specs, check_vma=False)
```

```python
import functools

import jax
import jax.numpy as jnp
from jax import lax
from jax.experimental import pallas as pl
from jax.experimental.pallas import tpu as pltpu
from jax.sharding import PartitionSpec as P

F32 = jnp.float32
BF16 = jnp.bfloat16
F16 = jnp.float16
TOP = 2.0**8
TAIL = 8
VMEM = pl.BlockSpec(memory_space=pltpu.VMEM)
SMEM = pl.BlockSpec(memory_space=pltpu.SMEM)
ANY = pl.BlockSpec(memory_space=pl.ANY)


def factors(peak):
    rows = lax.broadcasted_iota(jnp.int32, (TAIL, peak.shape[1]), 0)
    rest = peak
    table = jnp.ones((TAIL, peak.shape[1]), F32)
    scale = jnp.full_like(peak, TOP)
    for i in range(TAIL):
        large, small = rest > 2.0**7, rest < 2.0**-7
        up = jnp.where(large, 2.0**14, jnp.where(small, 2.0**-14, 1.0))
        down = jnp.where(large, 2.0**-14, jnp.where(small, 2.0**14, 1.0))
        rest = rest * down
        scale = scale * down
        table = jnp.where(rows == i, jnp.broadcast_to(up, table.shape), table)
    return table, scale


def product(table):
    whole = table[0:1]
    for i in range(1, TAIL):
        whole = whole * table[i : i + 1]
    return whole * (1.0 / TOP)


def peak_of(x):
    down = jnp.max(jnp.abs(x), axis=0, keepdims=True)
    return jnp.broadcast_to(jnp.max(down, axis=1, keepdims=True), down.shape)


def chain_of(parents, level, node):
    found = [None] * level
    for up in range(level - 1, -1, -1):
        node = parents[up, node]
        found[up] = node
    return found


def live_lanes(shape, size):
    return lax.broadcasted_iota(jnp.int32, shape, len(shape) - 1) < size


def base_kernel(npr, rows, width, place, sizes, whole_diag, out, message, marginal, diag, out_sem):
    row, col = place[0], place[1]
    bring = pltpu.make_async_copy(whole_diag.at[0], diag, out_sem)
    bring.start()
    bring.wait()
    for n in range(npr):
        value = diag_base(diag[n], sizes[0, row * npr + n], col * rows, rows, width)
        marginal[n] = value
        table, scale = factors(peak_of(value))
        message[n, :rows] = value * scale
        message[n, rows:] = table
    keep = pltpu.make_async_copy(marginal, out.at[0], out_sem)
    keep.start()
    keep.wait()


def diag_base(block, size, first, rows, width):
    lines = lax.broadcasted_iota(jnp.int32, (rows, width), 0) + first
    lanes = lax.broadcasted_iota(jnp.int32, (rows, width), 1)
    kept = jnp.where((lines < size) & (lanes < size), block, 0.0)
    return kept + jnp.where((lines == lanes) & (lines >= size), 1.0, 0.0)


def pack(turn, values, rows):
    high = values[0].shape[0]
    parts = []
    for value in values:
        table, scale = factors(peak_of(value))
        parts.append((value * scale, table))
    for c in range(turn.shape[0]):
        piece = slice(c * rows, (c + 1) * rows)
        turn[c, :high] = jnp.concatenate([v[:, piece] for v, _ in parts], axis=1)
        turn[c, high:] = jnp.concatenate([t[:, piece] for _, t in parts], axis=1)


def panel_moves(panel, off, lower, sem, col, n_col):
    def start(n, m):
        if len(panel) == 1:
            pltpu.make_async_copy(panel[0].at[:, off + m, n], lower.at[n, m], sem.at[n, m]).start()
            return
        z, core = lax.div(col, 2), lax.rem(col, 2)
        for i, piece in enumerate(panel):
            owner = lax.rem(z - i // 2 + n_col // 2, n_col // 2) * 2 + (core if i % 2 == 0 else 1 - core)
            pltpu.make_async_copy(piece.at[m, n], lower.at[n, m, owner], sem.at[n, m]).start()

    def wait(n, m):
        pltpu.make_async_copy(lower.at[n, m], lower.at[n, m], sem.at[n, m]).wait()

    return start, wait


def split_block(value, size, split, top_rows, low_rows):
    value = jnp.where(live_lanes(value.shape, size), value, 0.0)
    top = value.astype(BF16)
    split[top_rows] = top
    split[low_rows] = (value - top.astype(F32)).astype(BF16)


def upper_kernel(level, n_panel, off, n_wait, spans, n_row, npr, rows, width, *refs):
    place, parents, sizes = refs[:3]
    panel = refs[3 : 3 + n_panel]
    at = 3 + n_panel
    sources = []
    for up in range(level):
        parts = []
        for part in range(2):
            if (up, part) == (0, 0) or (up, part) == (level - 1, 1):
                parts.append(())
                continue
            parts.append(refs[at : at + spans[up]])
            at += spans[up]
        sources.append(parts)
    at += n_wait
    out, turn = refs[at : at + 2]
    lower, split, panel_sem, block_sem = refs[at + 2 : at + 6]
    holders = iter(refs[at + 6 :])
    row = place[0]
    high = (level - 1) * rows
    held = {
        (up, part): next(holders)
        for up in range(level)
        for part in range(2)
        if sources[up][part]
    }
    chains = [chain_of(parents, level, row * npr + n) for n in range(npr)]

    start, wait = panel_moves(panel, off, lower, panel_sem, place[1], lower.shape[2])

    for n in range(npr):
        for up in range(level):
            node = chains[n][up]
            back = lax.rem(row - lax.div(node, npr) + n_row, n_row)
            slot = lax.rem(node, npr)
            for part in range(2):
                for i, source in enumerate(sources[up][part]):

                    @pl.when(back == i)
                    def _():
                        pltpu.make_async_copy(
                            source.at[slot], held[up, part].at[n], block_sem.at[n, up, part]
                        ).start()
        for m in range(level):
            start(n, m)

    values = []
    for n in range(npr):
        live = [sizes[up, chains[n][up]] for up in range(level)]
        total = None
        for up in range(level):
            for part in range(2):
                if not sources[up][part]:
                    continue
                block = held[up, part]
                pltpu.make_async_copy(
                    sources[up][part][0].at[0], block.at[n], block_sem.at[n, up, part]
                ).wait()
                count = (block.shape[1] - TAIL) // rows
                whole = product(block[n, count * rows :])
                for b in range(count):
                    value = block[n, b * rows : (b + 1) * rows] * whole
                    l, m = (b, up) if up > 0 and part == 0 else (up, b)
                    split_block(
                        value,
                        live[m],
                        split,
                        (n, m, slice(l * rows, (l + 1) * rows)),
                        (n, m, slice(high + l * rows, high + (l + 1) * rows)),
                    )
        for m in range(level):
            wait(n, m)
            block = lower[n, m].reshape(width, width)
            term = jnp.dot(split[n, m], block, preferred_element_type=F32)
            total = term if total is None else total + term
        value = -(total[:high] + total[high:])
        values.append(jnp.where(live_lanes(value.shape, sizes[level, row * npr + n]), value, 0.0))
        out[n] = values[n]
    pack(turn, values, rows)


def cross_kernel(level, last, n_panel, off, n_source, n_wait, n_row, npr, rows, width, *refs):
    place, parents, sizes = refs[:3]
    panel = refs[3 : 3 + n_panel]
    sources = refs[3 + n_panel : 3 + n_panel + n_source]
    at = 3 + n_panel + n_source
    upper = None
    if level > 1:
        upper = refs[at]
        at += 1
    at += n_wait
    n_out = 2 if last else 3
    outs = refs[at : at + n_out]
    lower, split, held, panel_sem, block_sem, cross, out_sem = refs[at + n_out :]
    out, turn = outs[0], outs[1]
    passed = None if last else outs[2]
    row = place[0]
    high = level * rows
    chains = [chain_of(parents, level, row * npr + n) for n in range(npr)]

    start, wait = panel_moves(panel, off, lower, panel_sem, place[1], lower.shape[2])

    for n in range(npr):
        node = chains[n][level - 1]
        back = lax.rem(row - lax.div(node, npr) + n_row, n_row)
        for i, source in enumerate(sources):

            @pl.when(back == i)
            def _():
                pltpu.make_async_copy(
                    source.at[lax.rem(node, npr)], held.at[n], block_sem.at[n]
                ).start()

    for m in range(level):
        for n in range(npr):
            start(n, m)

    for n in range(npr):
        pltpu.make_async_copy(sources[0].at[0], held.at[n], block_sem.at[n]).wait()
        whole = product(held[n, high:])
        for m in range(level):
            split_block(
                held[n, m * rows : (m + 1) * rows] * whole,
                sizes[m, chains[n][m]],
                split,
                (n, m, slice(0, rows)),
                (n, m, slice(rows, 2 * rows)),
            )
    totals = [None] * npr
    for m in range(level):
        for n in range(npr):
            wait(n, m)
            block = lower[n, m].reshape(width, width)
            term = jnp.dot(split[n, m], block, preferred_element_type=F32)
            totals[n] = term if totals[n] is None else totals[n] + term
    values = []
    for n in range(npr):
        value = -(totals[n][:rows] + totals[n][rows:])
        values.append(jnp.where(live_lanes(value.shape, sizes[level, row * npr + n]), value, 0.0))
    for n in range(npr):
        cross[level - 1, n] = values[n]
        for l in range(level - 1):
            cross[l, n] = upper[n, l * rows : (l + 1) * rows]
    first = level * (level - 1) // 2
    keep = pltpu.make_async_copy(cross, out.at[first : first + level], out_sem)
    keep.start()
    pack(turn, values, rows)
    for n in range(npr):
        value = values[n]
        if level > 1:
            value = jnp.concatenate([upper[n], value], axis=0)
        if not last:
            table, scale = factors(peak_of(value))
            passed[n, :high] = value * scale
            passed[n, high:] = table
    keep.wait()


def marginal_kernel(level, last, n_panel, off, n_wait, n_row, npr, rows, width, *refs):
    place, sizes, diag = refs[:3]
    n_turned = min(level, 2)
    turned = refs[3 : 3 + n_turned]
    panel = refs[3 + n_turned : 3 + n_turned + n_panel]
    n_out = 1 if last else 2
    at = 3 + n_turned + n_panel + n_wait
    outs = refs[at : at + n_out]
    lower, panel_sem, marginal, out_sem = refs[at + n_out :]
    message = None if last else outs[1]
    row, col = place[0], place[1]
    n_col = lower.shape[2]
    high = level * rows

    start, wait = panel_moves(panel, off, lower, panel_sem, place[1], lower.shape[2])

    for m in range(level):
        for n in range(npr):
            start(n, m)

    def scales_of(part):
        lines = part.shape[1] - TAIL
        return jnp.concatenate(
            [jnp.broadcast_to(product(part[c, lines:]), (rows, npr * rows)) for c in range(n_col)], axis=0
        )

    scales = [scales_of(part) for part in turned]
    totals = [None] * npr
    sides = [[] for _ in range(npr)]
    for l in range(level):
        i, at_row = (n_turned - 1, 0) if l == level - 1 else (0, l * rows)
        upright = turned[i][:, at_row : at_row + rows].reshape(width, npr * rows) * scales[i]
        flat = upright.T
        top = flat.astype(BF16)
        low = (flat - top.astype(F32)).astype(BF16)
        for n in range(npr):
            mine = slice(n * rows, (n + 1) * rows)
            wait(n, l)
            block = lower[n, l].reshape(width, width)
            pair = jnp.concatenate([top[mine], low[mine]], axis=0)
            term = jnp.dot(pair, block, preferred_element_type=F32)
            term = term[:rows] + term[rows:]
            totals[n] = term if totals[n] is None else totals[n] + term
            sides[n].append(flat[mine])
    for n in range(npr):
        size = sizes[level, row * npr + n]
        value = diag_base(diag[n], size, col * rows, rows, width)
        value = value - jnp.where(live_lanes(value.shape, size), totals[n], 0.0)
        marginal[n] = value
        if n == npr - 1:
            keep = pltpu.make_async_copy(marginal, outs[0].at[level], out_sem)
            keep.start()
        if not last:
            peak = peak_of(value)
            for side in sides[n]:
                peak = jnp.maximum(peak, peak_of(side))
            table, scale = factors(peak)
            for l in range(level):
                message[n, l * rows : (l + 1) * rows] = sides[n][l] * scale
            message[n, high : high + rows] = value * scale
            message[n, high + rows :] = table
    keep.wait()


def gate_kernel(count, *refs):
    refs[count][...] = jnp.ones((1, 1, 1), F32)


def timing(rows_only, level, back):
    if level == 0 or (back == 1 and not rows_only):
        return ("due", level + 1) if back > 1 else ("free", -1)
    if rows_only:
        if back == 1:
            return "due", level
        return "due", (2 if level == 1 else level + max(back - 2, 0))
    return "due", (level + 1 if level == 1 else level + back - 1)


def params(limit=60 * 2**20):
    return pltpu.CompilerParams(vmem_limit_bytes=limit)


def shards(panel, diag_inverse, parents, supernode_sizes):
    levels, npr, rows, width = diag_inverse.shape
    n_row = lax.axis_size("row")
    n_col = lax.axis_size("col")
    place = jnp.stack([lax.axis_index("row"), lax.axis_index("col")]).astype(jnp.int32)

    def shape(*dims, dtype=F32):
        return jax.ShapeDtypeStruct(dims, dtype)

    def reach(level):
        return min(levels - 1 - level, n_row - 1)

    def gate(name, arrays):
        return pl.pallas_call(
            functools.partial(gate_kernel, len(arrays)),
            out_shape=shape(1, 1, 1),
            in_specs=[ANY] * len(arrays),
            out_specs=VMEM,
            name=name,
        )(*arrays)

    due = [[] for _ in range(levels)]
    gates = [[] for _ in range(levels)]

    def spread(message, level, rows_only):
        found = [message]
        half = message
        if rows_only and gates[level]:
            half = jnp.where(gate(f"gate{level}", gates[level]) > 0, message, 0.0)
        half = half.astype(F16)
        for back in range(1, reach(level) + 1):
            route = [(i, (i + back) % n_row) for i in range(n_row)]
            found.append(lax.ppermute(half, "row", route).astype(F32))
            where, when = timing(rows_only, level, back)
            {"due": due, "gate": gates, "free": due + [[]]}[where][when].append(found[-1])
        return found

    def turn_over(message):
        return lax.all_to_all(message.astype(F16), "col", 0, 0, tiled=True).astype(F32)

    def gathered(first, count, there):
        mine = jnp.where(there.astype(BF16).reshape(1, 1, 1, 1) > 0, panel[first : first + count], 0)
        return lax.all_gather(mine, "col", axis=0)

    def pieces(mine):
        swap = [(i, i ^ 1) for i in range(n_col)]
        found = []
        for back in range(n_col // 2):
            got = mine
            if back:
                got = lax.ppermute(mine, "col", [(i, (i + 2 * back) % n_col) for i in range(n_col)])
            found += [got, lax.ppermute(got, "col", swap)]
        return found

    whole_panel = [None] * levels
    whole_panel[1] = (pieces(panel[0:1]), 0)
    diagonals, message = pl.pallas_call(
        functools.partial(base_kernel, npr, rows, width),
        out_shape=(shape(levels, npr, rows, width), shape(npr, rows + TAIL, width)),
        in_specs=[SMEM, SMEM, ANY],
        out_specs=(ANY, VMEM),
        scratch_shapes=[
            pltpu.VMEM((npr, rows, width), F32),
            pltpu.VMEM((npr, rows, width), F32),
            pltpu.SemaphoreType.DMA(()),
        ],
        compiler_params=params(),
        name="base",
    )(place, supernode_sizes, diag_inverse)
    crosses = None
    table = [[(), spread(message, 0, False)]]

    def gather_level(level, there):
        first = level * (level - 1) // 2
        whole_panel[level] = ([gathered(first, level, there)], 0)

    there = gate("first", whole_panel[1][0][::2] + [message])
    for deeper in range(2, levels):
        gather_level(deeper, there)
    for level in range(1, levels):
        last = level == levels - 1
        high = level * rows
        whole, off = whole_panel[level]
        panel_scratch = [pltpu.VMEM((npr, level, n_col, rows, width), BF16)]
        upper = []
        turned = []
        if level > 1:
            spans = [min(level - up, n_row - 1) + 1 for up in range(level)]
            sources = []
            held = []
            for up in range(level):
                for part in range(2):
                    if (up, part) == (0, 0) or (up, part) == (level - 1, 1):
                        continue
                    sources.extend(table[up][part][: spans[up]])
                    held.append(pltpu.VMEM(table[up][part][0].shape, F32))
            upper = list(
                pl.pallas_call(
                    functools.partial(upper_kernel, level, len(whole), off, 1, spans, n_row, npr, rows, width),
                    out_shape=(
                        shape(npr, high - rows, width),
                        shape(n_col, high - rows + TAIL, npr * rows),
                    ),
                    in_specs=[SMEM, SMEM, SMEM] + [ANY] * (len(whole) + len(sources) + 1),
                    out_specs=(VMEM, VMEM),
                    scratch_shapes=panel_scratch
                    + [
                        pltpu.VMEM((npr, level, 2 * (high - rows), width), BF16),
                        pltpu.SemaphoreType.DMA((npr, level)),
                        pltpu.SemaphoreType.DMA((npr, level, 2)),
                    ]
                    + held,
                    compiler_params=params(),
                    name=f"upper{level}",
                )(place, parents, supernode_sizes, *whole, *sources, table[level - 1][1][0])
            )
            turned.append(turn_over(upper.pop()))
        newest = table[level - 1][1][: min(1, n_row - 1) + 1]
        waits = due[0] if level == 1 else []
        out_shape = [shape(panel.shape[0], npr, rows, width), shape(n_col, rows + TAIL, npr * rows)]
        if not last:
            out_shape.append(shape(npr, high + TAIL, width))
        before = [] if crosses is None else [crosses]
        n_given = 3 + len(whole) + len(newest) + len(upper) + len(waits)
        made = pl.pallas_call(
            functools.partial(
                cross_kernel, level, last, len(whole), off, len(newest), len(waits) + len(before), n_row, npr, rows, width
            ),
            out_shape=tuple(out_shape),
            in_specs=[SMEM, SMEM, SMEM] + [ANY] * (len(whole) + len(newest)) + [VMEM] * len(upper) + [ANY] * (len(waits) + len(before)),
            out_specs=(ANY,) + (VMEM,) * (len(out_shape) - 1),
            scratch_shapes=panel_scratch
            + [
                pltpu.VMEM((npr, level, 2 * rows, width), BF16),
                pltpu.VMEM((npr, high + TAIL, width), F32),
                pltpu.SemaphoreType.DMA((npr, level)),
                pltpu.SemaphoreType.DMA((npr,)),
                pltpu.VMEM((level, npr, rows, width), F32),
                pltpu.SemaphoreType.DMA(()),
            ],
            input_output_aliases={n_given: 0} if before else {},
            compiler_params=params(),
            cost_estimate=pl.CostEstimate(flops=4 * 10**10, bytes_accessed=2**20, transcendentals=0) if last else None,
            name=f"cross{level}",
        )(place, parents, supernode_sizes, *whole, *newest, *upper, *waits, *before)
        crosses = made[0]
        ahead = () if last else spread(made[2], level, True)
        newer = made[1]
        if last and turned:
            newer = jnp.where(gate(f"turn{level}", turned) > 0, newer, 0.0)
        turned.append(turn_over(newer))
        waits = [] if last else due[level] + whole_panel[level + 1][0]
        out_shape = [shape(levels, npr, rows, width)]
        if not last:
            out_shape.append(shape(npr, high + rows + TAIL, width))
        done = pl.pallas_call(
            functools.partial(marginal_kernel, level, last, len(whole), off, len(waits) + 1, n_row, npr, rows, width),
            out_shape=tuple(out_shape),
            in_specs=[SMEM, SMEM, VMEM] + [VMEM] * len(turned) + [ANY] * (len(whole) + len(waits) + 1),
            out_specs=(ANY,) + (VMEM,) * (len(out_shape) - 1),
            scratch_shapes=panel_scratch
            + [
                pltpu.SemaphoreType.DMA((npr, level)),
                pltpu.VMEM((npr, rows, width), F32),
                pltpu.SemaphoreType.DMA(()),
            ],
            input_output_aliases={3 + len(turned) + len(whole) + len(waits): 0},
            compiler_params=params(),
            name=f"marginal{level}",
        )(place, supernode_sizes, diag_inverse[level], *turned, *whole, *waits, diagonals)
        diagonals = done[0]
        if not last:
            table.append([ahead, spread(done[1], level, False)])
    return crosses, diagonals


def solution(mesh):
    in_specs = (P(None, "row", "col", None), P(None, "row", "col", None), P(), P())
    out_specs = (P(None, "row", "col", None), P(None, "row", "col", None))
    return jax.shard_map(shards, mesh=mesh, in_specs=in_specs, out_specs=out_specs, check_vma=False)
```

```python
import functools

import jax
import jax.numpy as jnp
from jax import lax
from jax.experimental import pallas as pl
from jax.experimental.pallas import tpu as pltpu
from jax.sharding import PartitionSpec as P

F32 = jnp.float32
BF16 = jnp.bfloat16
F16 = jnp.float16
TOP = 2.0**8
TAIL = 8
VMEM = pl.BlockSpec(memory_space=pltpu.VMEM)
SMEM = pl.BlockSpec(memory_space=pltpu.SMEM)
ANY = pl.BlockSpec(memory_space=pl.ANY)


def factors(peak):
    rows = lax.broadcasted_iota(jnp.int32, (TAIL, peak.shape[1]), 0)
    rest = peak
    table = jnp.ones((TAIL, peak.shape[1]), F32)
    scale = jnp.full_like(peak, TOP)
    for i in range(TAIL):
        large, small = rest > 2.0**7, rest < 2.0**-7
        up = jnp.where(large, 2.0**14, jnp.where(small, 2.0**-14, 1.0))
        down = jnp.where(large, 2.0**-14, jnp.where(small, 2.0**14, 1.0))
        rest = rest * down
        scale = scale * down
        table = jnp.where(rows == i, jnp.broadcast_to(up, table.shape), table)
    return table, scale


def product(table):
    whole = table[0:1]
    for i in range(1, TAIL):
        whole = whole * table[i : i + 1]
    return whole * (1.0 / TOP)


def peak_of(x):
    down = jnp.max(jnp.abs(x), axis=0, keepdims=True)
    return jnp.broadcast_to(jnp.max(down, axis=1, keepdims=True), down.shape)


def chain_of(parents, level, node):
    found = [None] * level
    for up in range(level - 1, -1, -1):
        node = parents[up, node]
        found[up] = node
    return found


def live_lanes(shape, size):
    return lax.broadcasted_iota(jnp.int32, shape, len(shape) - 1) < size


def base_kernel(npr, rows, width, place, sizes, whole_diag, out, message, marginal, diag, out_sem):
    row, col = place[0], place[1]
    bring = pltpu.make_async_copy(whole_diag.at[0], diag, out_sem)
    bring.start()
    bring.wait()
    for n in range(npr):
        value = diag_base(diag[n], sizes[0, row * npr + n], col * rows, rows, width)
        marginal[n] = value
        table, scale = factors(peak_of(value))
        message[n, :rows] = value * scale
        message[n, rows:] = table
    keep = pltpu.make_async_copy(marginal, out.at[0], out_sem)
    keep.start()
    keep.wait()


def diag_base(block, size, first, rows, width):
    lines = lax.broadcasted_iota(jnp.int32, (rows, width), 0) + first
    lanes = lax.broadcasted_iota(jnp.int32, (rows, width), 1)
    kept = jnp.where((lines < size) & (lanes < size), block, 0.0)
    return kept + jnp.where((lines == lanes) & (lines >= size), 1.0, 0.0)


def pack(turn, values, rows):
    high = values[0].shape[0]
    parts = []
    for value in values:
        table, scale = factors(peak_of(value))
        parts.append((value * scale, table))
    for c in range(turn.shape[0]):
        piece = slice(c * rows, (c + 1) * rows)
        turn[c, :high] = jnp.concatenate([v[:, piece] for v, _ in parts], axis=1)
        turn[c, high:] = jnp.concatenate([t[:, piece] for _, t in parts], axis=1)


def panel_moves(panel, off, lower, sem, col, n_col):
    def start(n, m):
        if len(panel) == 1:
            pltpu.make_async_copy(panel[0].at[:, off + m, n], lower.at[n, m], sem.at[n, m]).start()
            return
        z, core = lax.div(col, 2), lax.rem(col, 2)
        for i, piece in enumerate(panel):
            owner = lax.rem(z - i // 2 + n_col // 2, n_col // 2) * 2 + (core if i % 2 == 0 else 1 - core)
            pltpu.make_async_copy(piece.at[m, n], lower.at[n, m, owner], sem.at[n, m]).start()

    def wait(n, m):
        pltpu.make_async_copy(lower.at[n, m], lower.at[n, m], sem.at[n, m]).wait()

    return start, wait


def split_block(value, size, split, top_rows, low_rows):
    value = jnp.where(live_lanes(value.shape, size), value, 0.0)
    top = value.astype(BF16)
    split[top_rows] = top
    split[low_rows] = (value - top.astype(F32)).astype(BF16)


def upper_kernel(level, n_panel, off, n_wait, spans, n_row, npr, rows, width, *refs):
    place, parents, sizes = refs[:3]
    panel = refs[3 : 3 + n_panel]
    at = 3 + n_panel
    sources = []
    for up in range(level):
        parts = []
        for part in range(2):
            if (up, part) == (0, 0) or (up, part) == (level - 1, 1):
                parts.append(())
                continue
            parts.append(refs[at : at + spans[up]])
            at += spans[up]
        sources.append(parts)
    at += n_wait
    out, turn = refs[at : at + 2]
    lower, split, panel_sem, block_sem = refs[at + 2 : at + 6]
    holders = iter(refs[at + 6 :])
    row = place[0]
    high = (level - 1) * rows
    held = {
        (up, part): next(holders)
        for up in range(level)
        for part in range(2)
        if sources[up][part]
    }
    chains = [chain_of(parents, level, row * npr + n) for n in range(npr)]

    start, wait = panel_moves(panel, off, lower, panel_sem, place[1], lower.shape[2])

    for n in range(npr):
        for up in range(level):
            node = chains[n][up]
            back = lax.rem(row - lax.div(node, npr) + n_row, n_row)
            slot = lax.rem(node, npr)
            for part in range(2):
                for i, source in enumerate(sources[up][part]):

                    @pl.when(back == i)
                    def _():
                        pltpu.make_async_copy(
                            source.at[slot], held[up, part].at[n], block_sem.at[n, up, part]
                        ).start()
        for m in range(level):
            start(n, m)

    values = []
    for n in range(npr):
        live = [sizes[up, chains[n][up]] for up in range(level)]
        total = None
        for up in range(level):
            for part in range(2):
                if not sources[up][part]:
                    continue
                block = held[up, part]
                pltpu.make_async_copy(
                    sources[up][part][0].at[0], block.at[n], block_sem.at[n, up, part]
                ).wait()
                count = (block.shape[1] - TAIL) // rows
                whole = product(block[n, count * rows :])
                for b in range(count):
                    value = block[n, b * rows : (b + 1) * rows] * whole
                    l, m = (b, up) if up > 0 and part == 0 else (up, b)
                    split_block(
                        value,
                        live[m],
                        split,
                        (n, m, slice(l * rows, (l + 1) * rows)),
                        (n, m, slice(high + l * rows, high + (l + 1) * rows)),
                    )
        for m in range(level):
            wait(n, m)
            block = lower[n, m].reshape(width, width)
            term = jnp.dot(split[n, m], block, preferred_element_type=F32)
            total = term if total is None else total + term
        value = -(total[:high] + total[high:])
        values.append(jnp.where(live_lanes(value.shape, sizes[level, row * npr + n]), value, 0.0))
        out[n] = values[n]
    pack(turn, values, rows)


def cross_kernel(level, last, n_panel, off, n_source, n_wait, n_row, npr, rows, width, *refs):
    place, parents, sizes = refs[:3]
    panel = refs[3 : 3 + n_panel]
    sources = refs[3 + n_panel : 3 + n_panel + n_source]
    at = 3 + n_panel + n_source
    upper = None
    if level > 1:
        upper = refs[at]
        at += 1
    at += n_wait
    n_out = 2 if last else 3
    outs = refs[at : at + n_out]
    lower, split, held, panel_sem, block_sem, cross, out_sem = refs[at + n_out :]
    out, turn = outs[0], outs[1]
    passed = None if last else outs[2]
    row = place[0]
    high = level * rows
    chains = [chain_of(parents, level, row * npr + n) for n in range(npr)]

    start, wait = panel_moves(panel, off, lower, panel_sem, place[1], lower.shape[2])

    for n in range(npr):
        node = chains[n][level - 1]
        back = lax.rem(row - lax.div(node, npr) + n_row, n_row)
        for i, source in enumerate(sources):

            @pl.when(back == i)
            def _():
                pltpu.make_async_copy(
                    source.at[lax.rem(node, npr)], held.at[n], block_sem.at[n]
                ).start()

    for m in range(level):
        for n in range(npr):
            start(n, m)

    for n in range(npr):
        pltpu.make_async_copy(sources[0].at[0], held.at[n], block_sem.at[n]).wait()
        whole = product(held[n, high:])
        for m in range(level):
            split_block(
                held[n, m * rows : (m + 1) * rows] * whole,
                sizes[m, chains[n][m]],
                split,
                (n, m, slice(0, rows)),
                (n, m, slice(rows, 2 * rows)),
            )
    totals = [None] * npr
    for m in range(level):
        for n in range(npr):
            wait(n, m)
            block = lower[n, m].reshape(width, width)
            term = jnp.dot(split[n, m], block, preferred_element_type=F32)
            totals[n] = term if totals[n] is None else totals[n] + term
    values = []
    for n in range(npr):
        value = -(totals[n][:rows] + totals[n][rows:])
        values.append(jnp.where(live_lanes(value.shape, sizes[level, row * npr + n]), value, 0.0))
    for n in range(npr):
        cross[level - 1, n] = values[n]
        for l in range(level - 1):
            cross[l, n] = upper[n, l * rows : (l + 1) * rows]
    first = level * (level - 1) // 2
    keep = pltpu.make_async_copy(cross, out.at[first : first + level], out_sem)
    keep.start()
    pack(turn, values, rows)
    for n in range(npr):
        value = values[n]
        if level > 1:
            value = jnp.concatenate([upper[n], value], axis=0)
        if not last:
            table, scale = factors(peak_of(value))
            passed[n, :high] = value * scale
            passed[n, high:] = table
    keep.wait()


def scales_of(part, rows):
    lines = part.shape[1] - TAIL
    return jnp.concatenate(
        [jnp.broadcast_to(product(part[c, lines:]), (rows, part.shape[2])) for c in range(part.shape[0])], axis=0
    )


def flat_terms(part, at_row, scale, rows, width):
    flat = (part[:, at_row : at_row + rows].reshape(width, part.shape[2]) * scale).T
    top = flat.astype(BF16)
    return flat, top, (flat - top.astype(F32)).astype(BF16)


def against(top, low, mine, block, rows):
    pair = jnp.concatenate([top[mine], low[mine]], axis=0)
    term = jnp.dot(pair, block, preferred_element_type=F32)
    return term[:rows] + term[rows:]


def partial_kernel(level, off, npr, rows, width, place, turned, panel, out, lower, panel_sem):
    start, wait = panel_moves([panel], off, lower, panel_sem, place[1], lower.shape[2])
    for m in range(level - 1):
        for n in range(npr):
            start(n, m)
    scale = scales_of(turned, rows)
    totals = [None] * npr
    for l in range(level - 1):
        _, top, low = flat_terms(turned, l * rows, scale, rows, width)
        for n in range(npr):
            wait(n, l)
            mine = slice(n * rows, (n + 1) * rows)
            term = against(top, low, mine, lower[n, l].reshape(width, width), rows)
            totals[n] = term if totals[n] is None else totals[n] + term
    for n in range(npr):
        out[n] = totals[n]


def marginal_kernel(level, last, n_panel, off, n_wait, n_row, npr, rows, width, *refs):
    place, sizes, diag = refs[:3]
    n_turned = min(level, 2)
    turned = refs[3 : 3 + n_turned]
    panel = refs[3 + n_turned : 3 + n_turned + n_panel]
    n_out = 1 if last else 2
    at = 3 + n_turned + n_panel + n_wait
    outs = refs[at : at + n_out]
    lower, panel_sem, marginal, out_sem = refs[at + n_out :]
    message = None if last else outs[1]
    row, col = place[0], place[1]
    n_col = lower.shape[2]
    high = level * rows

    start, wait = panel_moves(panel, off, lower, panel_sem, place[1], lower.shape[2])

    todo = range(level)
    totals = [None] * npr
    if last and level > 1:
        todo = range(level - 1, level)
        totals = [turned[0][n] for n in range(npr)]
    for m in todo:
        for n in range(npr):
            start(n, m)

    scales = [None if len(todo) < level and i == 0 else scales_of(part, rows) for i, part in enumerate(turned)]
    sides = [[] for _ in range(npr)]
    for l in todo:
        i, at_row = (n_turned - 1, 0) if l == level - 1 else (0, l * rows)
        flat, top, low = flat_terms(turned[i], at_row, scales[i], rows, width)
        for n in range(npr):
            mine = slice(n * rows, (n + 1) * rows)
            wait(n, l)
            term = against(top, low, mine, lower[n, l].reshape(width, width), rows)
            totals[n] = term if totals[n] is None else totals[n] + term
            sides[n].append(flat[mine])
    for n in range(npr):
        size = sizes[level, row * npr + n]
        value = diag_base(diag[n], size, col * rows, rows, width)
        value = value - jnp.where(live_lanes(value.shape, size), totals[n], 0.0)
        marginal[n] = value
        if n == npr - 1:
            keep = pltpu.make_async_copy(marginal, outs[0].at[level], out_sem)
            keep.start()
        if not last:
            peak = peak_of(value)
            for side in sides[n]:
                peak = jnp.maximum(peak, peak_of(side))
            table, scale = factors(peak)
            for l in range(level):
                message[n, l * rows : (l + 1) * rows] = sides[n][l] * scale
            message[n, high : high + rows] = value * scale
            message[n, high + rows :] = table
    keep.wait()


def gate_kernel(count, *refs):
    refs[count][...] = jnp.ones((1, 1, 1), F32)


def timing(rows_only, level, back):
    if level == 0 or (back == 1 and not rows_only):
        return ("due", level + 1) if back > 1 else ("free", -1)
    if rows_only:
        if back == 1:
            return "due", level
        return "due", (2 if level == 1 else level + max(back - 2, 0))
    return "due", (level + 1 if level == 1 else level + back - 1)


def params(limit=60 * 2**20):
    return pltpu.CompilerParams(vmem_limit_bytes=limit)


def shards(panel, diag_inverse, parents, supernode_sizes):
    levels, npr, rows, width = diag_inverse.shape
    n_row = lax.axis_size("row")
    n_col = lax.axis_size("col")
    place = jnp.stack([lax.axis_index("row"), lax.axis_index("col")]).astype(jnp.int32)

    def shape(*dims, dtype=F32):
        return jax.ShapeDtypeStruct(dims, dtype)

    def reach(level):
        return min(levels - 1 - level, n_row - 1)

    def gate(name, arrays):
        return pl.pallas_call(
            functools.partial(gate_kernel, len(arrays)),
            out_shape=shape(1, 1, 1),
            in_specs=[ANY] * len(arrays),
            out_specs=VMEM,
            name=name,
        )(*arrays)

    due = [[] for _ in range(levels)]
    gates = [[] for _ in range(levels)]

    def spread(message, level, rows_only):
        found = [message]
        half = message
        if rows_only and gates[level]:
            half = jnp.where(gate(f"gate{level}", gates[level]) > 0, message, 0.0)
        half = half.astype(F16)
        for back in range(1, reach(level) + 1):
            route = [(i, (i + back) % n_row) for i in range(n_row)]
            found.append(lax.ppermute(half, "row", route).astype(F32))
            where, when = timing(rows_only, level, back)
            {"due": due, "gate": gates, "free": due + [[]]}[where][when].append(found[-1])
        return found

    def turn_over(message):
        return lax.all_to_all(message.astype(F16), "col", 0, 0, tiled=True).astype(F32)

    def gathered(first, count, there):
        mine = jnp.where(there.astype(BF16).reshape(1, 1, 1, 1) > 0, panel[first : first + count], 0)
        return lax.all_gather(mine, "col", axis=0)

    def pieces(mine):
        swap = [(i, i ^ 1) for i in range(n_col)]
        found = []
        for back in range(n_col // 2):
            got = mine
            if back:
                got = lax.ppermute(mine, "col", [(i, (i + 2 * back) % n_col) for i in range(n_col)])
            found += [got, lax.ppermute(got, "col", swap)]
        return found

    whole_panel = [None] * levels
    whole_panel[1] = (pieces(panel[0:1]), 0)
    diagonals, message = pl.pallas_call(
        functools.partial(base_kernel, npr, rows, width),
        out_shape=(shape(levels, npr, rows, width), shape(npr, rows + TAIL, width)),
        in_specs=[SMEM, SMEM, ANY],
        out_specs=(ANY, VMEM),
        scratch_shapes=[
            pltpu.VMEM((npr, rows, width), F32),
            pltpu.VMEM((npr, rows, width), F32),
            pltpu.SemaphoreType.DMA(()),
        ],
        compiler_params=params(),
        name="base",
    )(place, supernode_sizes, diag_inverse)
    crosses = None
    table = [[(), spread(message, 0, False)]]

    def gather_level(level, there):
        first = level * (level - 1) // 2
        whole_panel[level] = ([gathered(first, level, there)], 0)

    there = gate("first", whole_panel[1][0][::2] + [message])
    for deeper in range(2, levels):
        gather_level(deeper, there)
    for level in range(1, levels):
        last = level == levels - 1
        high = level * rows
        whole, off = whole_panel[level]
        panel_scratch = [pltpu.VMEM((npr, level, n_col, rows, width), BF16)]
        upper = []
        turned = []
        if level > 1:
            spans = [min(level - up, n_row - 1) + 1 for up in range(level)]
            sources = []
            held = []
            for up in range(level):
                for part in range(2):
                    if (up, part) == (0, 0) or (up, part) == (level - 1, 1):
                        continue
                    sources.extend(table[up][part][: spans[up]])
                    held.append(pltpu.VMEM(table[up][part][0].shape, F32))
            upper = list(
                pl.pallas_call(
                    functools.partial(upper_kernel, level, len(whole), off, 1, spans, n_row, npr, rows, width),
                    out_shape=(
                        shape(npr, high - rows, width),
                        shape(n_col, high - rows + TAIL, npr * rows),
                    ),
                    in_specs=[SMEM, SMEM, SMEM] + [ANY] * (len(whole) + len(sources) + 1),
                    out_specs=(VMEM, VMEM),
                    scratch_shapes=panel_scratch
                    + [
                        pltpu.VMEM((npr, level, 2 * (high - rows), width), BF16),
                        pltpu.SemaphoreType.DMA((npr, level)),
                        pltpu.SemaphoreType.DMA((npr, level, 2)),
                    ]
                    + held,
                    compiler_params=params(),
                    name=f"upper{level}",
                )(place, parents, supernode_sizes, *whole, *sources, table[level - 1][1][0])
            )
            turned.append(turn_over(upper.pop()))
        newest = table[level - 1][1][: min(1, n_row - 1) + 1]
        waits = due[0] if level == 1 else []
        out_shape = [shape(panel.shape[0], npr, rows, width), shape(n_col, rows + TAIL, npr * rows)]
        if not last:
            out_shape.append(shape(npr, high + TAIL, width))
        before = [] if crosses is None else [crosses]
        n_given = 3 + len(whole) + len(newest) + len(upper) + len(waits)
        made = pl.pallas_call(
            functools.partial(
                cross_kernel, level, last, len(whole), off, len(newest), len(waits) + len(before), n_row, npr, rows, width
            ),
            out_shape=tuple(out_shape),
            in_specs=[SMEM, SMEM, SMEM] + [ANY] * (len(whole) + len(newest)) + [VMEM] * len(upper) + [ANY] * (len(waits) + len(before)),
            out_specs=(ANY,) + (VMEM,) * (len(out_shape) - 1),
            scratch_shapes=panel_scratch
            + [
                pltpu.VMEM((npr, level, 2 * rows, width), BF16),
                pltpu.VMEM((npr, high + TAIL, width), F32),
                pltpu.SemaphoreType.DMA((npr, level)),
                pltpu.SemaphoreType.DMA((npr,)),
                pltpu.VMEM((level, npr, rows, width), F32),
                pltpu.SemaphoreType.DMA(()),
            ],
            input_output_aliases={n_given: 0} if before else {},
            compiler_params=params(),
            cost_estimate=pl.CostEstimate(flops=4 * 10**10, bytes_accessed=2**20, transcendentals=0) if last else None,
            name=f"cross{level}",
        )(place, parents, supernode_sizes, *whole, *newest, *upper, *waits, *before)
        crosses = made[0]
        ahead = () if last else spread(made[2], level, True)
        newer = made[1]
        if last and turned:
            newer = jnp.where(gate(f"turn{level}", turned) > 0, newer, 0.0)
        if last and turned:
            turned = [
                pl.pallas_call(
                    functools.partial(partial_kernel, level, off, npr, rows, width),
                    out_shape=shape(npr, rows, width),
                    in_specs=[SMEM, VMEM, ANY],
                    out_specs=VMEM,
                    scratch_shapes=panel_scratch + [pltpu.SemaphoreType.DMA((npr, level))],
                    compiler_params=params(),
                    name=f"partial{level}",
                )(place, turned[0], *whole)
            ]
        turned.append(turn_over(newer))
        waits = [] if last else due[level] + whole_panel[level + 1][0]
        out_shape = [shape(levels, npr, rows, width)]
        if not last:
            out_shape.append(shape(npr, high + rows + TAIL, width))
        done = pl.pallas_call(
            functools.partial(marginal_kernel, level, last, len(whole), off, len(waits) + 1, n_row, npr, rows, width),
            out_shape=tuple(out_shape),
            in_specs=[SMEM, SMEM, VMEM] + [VMEM] * len(turned) + [ANY] * (len(whole) + len(waits) + 1),
            out_specs=(ANY,) + (VMEM,) * (len(out_shape) - 1),
            scratch_shapes=panel_scratch
            + [
                pltpu.SemaphoreType.DMA((npr, level)),
                pltpu.VMEM((npr, rows, width), F32),
                pltpu.SemaphoreType.DMA(()),
            ],
            input_output_aliases={3 + len(turned) + len(whole) + len(waits): 0},
            compiler_params=params(),
            name=f"marginal{level}",
        )(place, supernode_sizes, diag_inverse[level], *turned, *whole, *waits, diagonals)
        diagonals = done[0]
        if not last:
            table.append([ahead, spread(done[1], level, False)])
    return crosses, diagonals


def solution(mesh):
    in_specs = (P(None, "row", "col", None), P(None, "row", "col", None), P(), P())
    out_specs = (P(None, "row", "col", None), P(None, "row", "col", None))
    return jax.shard_map(shards, mesh=mesh, in_specs=in_specs, out_specs=out_specs, check_vma=False)
```
